512 devices in a mesh: dom: 64 (over z_lo, x, core), rep: 8 (over z_hi, y).
Axes of the slice: x: 4, y: 4, z: 16 (z_hi: 2, z_lo: 8; z = z_hi * 8 + z_lo), core: 2. Of those that a mesh axis runs over, the one named last changes fastest.
Arguments:
- features: bfloat16 [65536, 512], P('dom'), may hold values from -6 to 6
- tiles: bfloat16 [24576, 128, 128], P(('dom', 'rep')), may hold values from -0.078125 to 0.078125
- tile_rows: int32 [24576], P(('dom', 'rep')), may hold values from 0 to 7
- tile_cols: int32 [24576], P(('dom', 'rep')), may hold values from 0 to 511, as said below
- tile_count: int32 [512], P(('dom', 'rep')), may hold values from 6 to 48, as said below
- weight: bfloat16 [512, 512], replicated, may hold values from -0.25 to 0.25
- cotangent: bfloat16 [65536, 512], P(('dom', 'rep')), may hold values from -6 to 6
Outputs:
- node_out: bfloat16 [65536, 512], P(('dom', 'rep'))
- weight_grad: float32 [512, 512], replicated
The draws below stay inside these ranges and needn't reach their ends.
Inputs may be any that keep to these rules, and one draw needn't show every extreme that they name: Each device holds distinct (tile_rows, tile_cols) pairs; the slots of device d = p * 8 + r name tile columns of the 8 partitions q with (p - r - q) mod 64 divisible by 8. `tile_count`: some device uses all its slots.
All inputs are finite; a program needn't handle non-finite values.
Results may differ from the reference program's by a relative error of at most 0.015.
Values may be sent and summed in bfloat16 or wider, within the bound.
A program may use at most 64 MiB of HBM per device.

```python
import jax
import jax.numpy as jnp
from jax import lax

F = 512
TILE = 128
TROWS = 8
TILES_DEV = 48
STEPS = 8
NT = 512
NODES = 65536
SLOTS = 24576
N_DOM = 64
N_REP = 8
DEVICES = 512


def place_tiles(key):
    spots = STEPS * TROWS * TROWS
    keys = jax.random.split(key, DEVICES)

    def pick(single):
        return jax.random.permutation(single, spots)[:TILES_DEV]
    chosen = jax.vmap(pick)(keys).astype(jnp.int32)
    source_step = chosen // (TROWS * TROWS)
    within = chosen % (TROWS * TROWS)
    row_tile = within // TROWS
    col_tile = within % TROWS
    device = jnp.arange(DEVICES, dtype=jnp.int32)[:, None]
    owner = device // N_REP
    member = device % N_REP
    source = (owner - member - N_REP * source_step) % N_DOM
    return (row_tile.reshape(-1), (source * TROWS + col_tile).reshape(-1))


def draw_tile_rows(key, part):
    placed = place_tiles(key)
    return placed[0].astype(jnp.int32)


def draw_tile_cols(key, part):
    placed = place_tiles(key)
    return placed[1].astype(jnp.int32)


def draw_tile_count(key, part):
    key = jax.random.fold_in(key, 7)
    spread = jax.random.randint(key, (DEVICES,), 0, TILES_DEV + 1)
    counts = TILES_DEV // 8 + spread * spread // TILES_DEV
    counts = jnp.minimum(counts, TILES_DEV)
    fullest = jax.random.randint(jax.random.fold_in(key, 1), (), 0, DEVICES)
    counts = jnp.where(jnp.arange(DEVICES) == fullest, TILES_DEV, counts)
    return counts.astype(jnp.int32)


def levels(stream_key, shape, cuts, low, top_value):
    factor_of, own = 1.0, jax.random.fold_in(stream_key, 6)
    for dim, shards_of in cuts:
        draws = jnp.exp(jax.random.uniform(jax.random.fold_in(own, dim), (shards_of,), jnp.float32, low / len(cuts), top_value / len(cuts)))
        factor_of = factor_of * jnp.repeat(draws, shape[dim] // shards_of).reshape([-1 if axis == dim else 1 for axis in range(len(shape))])
    return factor_of


def normal_values(key, dims, deviation, limit, cuts=(), held_as=jnp.bfloat16):
    level = levels(key, dims, cuts, -0.22, 0.18) if cuts else 1.0
    array = jax.random.normal(key, dims, jnp.float32) * deviation * level
    return jnp.minimum(jnp.maximum(array, -limit), limit).astype(held_as)


def setup_inputs(seed: int = 0) -> dict:
    key_list = jax.random.split(jax.random.key(seed), 8)
    features = normal_values(key_list[0], (NODES, F), 1.0, 6.0, ((0, 64),))
    tiles = normal_values(key_list[1], (SLOTS, TILE, TILE), (N_REP * TILES_DEV * TILE // TROWS) ** -0.5, 0.078125, ((0, 512),))
    tile_rows = draw_tile_rows(jax.random.fold_in(key_list[7], 71), 0)
    tile_cols = draw_tile_cols(jax.random.fold_in(key_list[7], 71), 0)
    tile_count = draw_tile_count(jax.random.fold_in(key_list[7], 71), 0)
    weight = normal_values(key_list[5], (F, F), F ** -0.5, 0.25)
    cotangent = normal_values(key_list[6], (NODES, F), 1.0, 6.0, ((0, 512),))
    return {"features": features, "tiles": tiles, "tile_rows": tile_rows, "tile_cols": tile_cols, "tile_count": tile_count, "weight": weight, "cotangent": cotangent}


def reference(features, tiles, tile_rows, tile_cols, tile_count, weight, cotangent):
    tile_size = tiles.shape[1]
    width = features.shape[1]
    blocks = features.reshape(NT, tile_size, width)
    tile_sets = tiles.reshape(DEVICES, TILES_DEV, tile_size, tile_size)
    row_sets = tile_rows.reshape(DEVICES, TILES_DEV)
    col_sets = tile_cols.reshape(DEVICES, TILES_DEV)
    devices = jnp.arange(DEVICES).astype(jnp.int32)
    rows_block = TROWS * tile_size

    def one_device(carry, items):
        tile_set, row_set, col_set, live_count, device = items
        inputs = blocks[col_set].astype(jnp.float32)
        products = jnp.einsum("sij,sjf->sif", tile_set.astype(jnp.float32), inputs)
        live_slots = jnp.arange(TILES_DEV) < live_count
        placing = ((row_set[:, None] == jnp.arange(TROWS)[None, :]) & live_slots[:, None]).astype(jnp.float32)
        partial_sum = jnp.einsum("st,sif->tif", placing, products).reshape(rows_block, width)
        start = ((device // N_REP) * rows_block).astype(jnp.int32)
        current = lax.dynamic_slice_in_dim(carry, start, rows_block, 0)
        carry = lax.dynamic_update_slice_in_dim(carry, current + partial_sum, start, 0)
        return carry, None

    initial = jnp.zeros((NODES, width), jnp.float32)
    aggregate, unused = lax.scan(one_device, initial, (tile_sets, row_sets, col_sets, tile_count, devices))
    aggregated = aggregate.astype(jnp.bfloat16)
    pre = jnp.dot(aggregated, weight, preferred_element_type=jnp.float32)
    sigma = jax.nn.sigmoid(pre)
    node_out = (pre * sigma).astype(jnp.bfloat16)
    slope = (cotangent.astype(jnp.float32) * sigma * (1.0 + pre * (1.0 - sigma))).astype(jnp.bfloat16)
    weight_grad = jnp.dot(aggregated.T, slope, preferred_element_type=jnp.float32)
    return node_out, weight_grad
```

```python
import functools

import jax
import jax.numpy as jnp
from jax import lax
from jax.experimental import pallas as pl
from jax.experimental.pallas import tpu as pltpu
from jax.sharding import PartitionSpec as P

MESH = pl.DeviceIdType.MESH
BF16 = jnp.bfloat16
F32 = jnp.float32


def at(x, y, zl, zh, core):
    return zl * 8 + x * 2 + core, zh * 4 + y


def hosted(x, y, zh, core):
    c = (2 * x + core + 16 - 4 * zh - y) % 8
    natural, natural_core = c // 2, c % 2
    b = (x + 8 - natural - 2 * zh) % 4
    host_x = (x + b + 3) % 4
    side = ((host_x + 4 - natural) % 4 - 1) // 2
    host_y = natural_core * (1 - side) + (1 - natural_core) * (2 + side)
    return host_x, host_y


def class_of(host_y):
    natural_core = 1 - host_y // 2
    side = natural_core * (1 - host_y) + (1 - natural_core) * (host_y - 2)
    return side, natural_core


def set_of(host_x, host_y, zh, core):
    side, natural_core = class_of(host_y)
    moved = (side + zh) % 2
    right = 1 - natural_core * (1 - core) * 2
    x = (host_x + 4 + moved * right) % 4
    low = (1 - natural_core) * core + natural_core * (1 - core) * 3
    high = (1 - natural_core) * (2 + core) + natural_core * (1 + core)
    return x, moved * low + (1 - moved) * high


def place():
    dom, rep = lax.axis_index("dom"), lax.axis_index("rep")
    return (dom // 2) % 4, rep % 4, dom // 8, rep // 4, dom % 2


def z_neighbour(x, y, zl, zh, core, distance):
    z = (zh * 8 + zl + distance + 16) % 16
    return at(x, y, z % 8, z // 8, core)


def signal(device):
    pl.semaphore_signal(pltpu.get_barrier_semaphore(), inc=1, device_id=device, device_id_type=MESH)


UNITS = 2


def gather_kernel(features, blocks, own_send, own_recv, up_send, up_recv, down_send, down_recv, pair_send, pair_recv):
    x, y, zl, zh, core = place()
    side, natural_core = class_of(y)
    up = z_neighbour(x, y, zl, zh, core, 1)
    down = z_neighbour(x, y, zl, zh, core, -1)
    sibling = at(x, y, zl, zh, 1 - core)
    source = at((x + 3 + 2 * side) % 4, y, zl, zh, natural_core)
    target_x = (x + 1 + 2 * side) % 4
    half = features.shape[0] // 2
    unit = half // UNITS

    for device in (up, down, sibling, source):
        signal(device)

    @pl.when(core == natural_core)
    def _():
        pl.semaphore_wait(pltpu.get_barrier_semaphore(), 5)

    @pl.when(core != natural_core)
    def _():
        pl.semaphore_wait(pltpu.get_barrier_semaphore(), 3)

    def rows(h, of_core):
        return pl.ds(pl.multiple_of(of_core * half + h * unit, unit), unit)

    def part(distance, h, of_core):
        return blocks.at[(zl + distance + 8) % 8, rows(h, of_core)]

    def own_copy(h, to_core):
        return pltpu.make_async_remote_copy(
            src_ref=features.at[rows(h, to_core)],
            dst_ref=part(0, h, to_core),
            send_sem=own_send.at[h, to_core],
            recv_sem=own_recv.at[h],
            device_id=at(target_x, y, zl, zh, to_core),
            device_id_type=MESH,
        )

    @pl.when(core == natural_core)
    def _():
        for h in range(UNITS):
            for to_core in range(2):
                own_copy(h, to_core).start()

    def hop(step, h, upward):
        ref = part(-step if upward else step, h, core)
        send, recv = (up_send, up_recv) if upward else (down_send, down_recv)
        return pltpu.make_async_remote_copy(
            src_ref=ref,
            dst_ref=ref,
            send_sem=send.at[step, h],
            recv_sem=recv.at[step, h],
            device_id=up if upward else down,
            device_id_type=MESH,
        )

    def arrival(step, h, upward):
        ref = part(-step - 1 if upward else step + 1, h, core)
        send, recv = (up_send, up_recv) if upward else (down_send, down_recv)
        return pltpu.make_async_remote_copy(
            src_ref=ref,
            dst_ref=ref,
            send_sem=send.at[step, h],
            recv_sem=recv.at[step, h],
            device_id=up if upward else down,
            device_id_type=MESH,
        )

    def to_sibling(distance, h):
        ref = part(distance, h, core)
        return pltpu.make_async_remote_copy(
            src_ref=ref,
            dst_ref=ref,
            send_sem=pair_send.at[distance + 4, h],
            recv_sem=pair_recv.at[distance + 4, h],
            device_id=sibling,
            device_id_type=MESH,
        )

    def from_sibling(distance, h):
        ref = part(distance, h, 1 - core)
        return pltpu.make_async_remote_copy(
            src_ref=ref,
            dst_ref=ref,
            send_sem=pair_send.at[distance + 4, h],
            recv_sem=pair_recv.at[distance + 4, h],
            device_id=sibling,
            device_id_type=MESH,
        )

    def last(h, upward):
        return 4 if (h < UNITS // 2) == upward else 3

    for h in range(UNITS):
        own_copy(h, 0).wait_recv()
        hop(0, h, True).start()
        hop(0, h, False).start()
        to_sibling(0, h).start()
    for step in range(4):
        for h in range(UNITS):
            for upward in (True, False):
                if step < last(h, upward):
                    arrival(step, h, upward).wait_recv()
                    if step + 1 < last(h, upward):
                        hop(step + 1, h, upward).start()
                    distance = -step - 1 if upward else step + 1
                    if distance == 4:
                        distance = -4
                    to_sibling(distance, h).start()
    for distance in range(-4, 4):
        for h in range(UNITS):
            from_sibling(distance, h).wait_recv()
    for distance in range(-4, 4):
        for h in range(UNITS):
            to_sibling(distance, h).wait_send()
    for step in range(4):
        for h in range(UNITS):
            for upward in (True, False):
                if step < last(h, upward):
                    hop(step, h, upward).wait_send()

    @pl.when(core == natural_core)
    def _():
        for h in range(UNITS):
            for to_core in range(2):
                own_copy(h, to_core).wait_send()


def gather(features):
    nodes, width = features.shape
    sems = pltpu.SemaphoreType.DMA
    return pl.pallas_call(
        gather_kernel,
        out_shape=jax.ShapeDtypeStruct((8, nodes, width), features.dtype),
        in_specs=[pl.BlockSpec(memory_space=pl.ANY)],
        out_specs=pl.BlockSpec(memory_space=pl.ANY),
        scratch_shapes=[
            sems((UNITS, 2)),
            sems((UNITS,)),
            sems((4, UNITS)),
            sems((4, UNITS)),
            sems((4, UNITS)),
            sems((4, UNITS)),
            sems((8, UNITS)),
            sems((8, UNITS)),
        ],
        compiler_params=pltpu.CompilerParams(collective_id=0, has_side_effects=True),
        name="gather",
    )(features)


def tile_kernel(rows, cols, count, tiles, blocks, out, total):
    total[...] = jnp.zeros_like(total)

    def one(slot, carry):
        col = cols[slot]
        block = blocks[(col // 64) * 8 + col % 8]
        total[rows[slot]] += jnp.dot(tiles[slot], block, preferred_element_type=F32)
        return carry

    lax.fori_loop(0, count[0], one, 0)
    out[...] = total[...].astype(out.dtype)


def tile_products(rows, cols, count, tiles, blocks):
    width = blocks.shape[-1]
    smem = pl.BlockSpec(memory_space=pltpu.SMEM)
    vmem = pl.BlockSpec(memory_space=pltpu.VMEM)
    return pl.pallas_call(
        tile_kernel,
        out_shape=jax.ShapeDtypeStruct((8, 128, width), BF16),
        in_specs=[smem, smem, smem, vmem, vmem],
        out_specs=vmem,
        scratch_shapes=[pltpu.VMEM((8, 128, width), F32)],
        compiler_params=pltpu.CompilerParams(vmem_limit_bytes=40 * 2**20),
        name="tile_products",
    )(rows, cols, count, tiles, blocks)


def finish_kernel(
    partial, weight, cotangent, node_out, weight_grad,
    plane_in, z_in, z_out, agg, slope, grad, grad_in, piece, piece_in, total, total_in, whole,
    plane_send, plane_recv, z_sems, agg_sems, slope_sems, grad_send, grad_recv,
    piece_send, piece_recv, total_send, total_recv, whole_send, whole_recv, last_sems,
):
    x, y, zl, zh, core = place()
    z = zh * 8 + zl
    spot = x * 4 + y
    sibling = at(x, y, zl, zh, 1 - core)

    def in_plane(distance):
        there = (spot + distance) % 16
        return at(there // 4, there % 4, zl, zh, core)

    for distance in range(1, 16):
        signal(in_plane(distance))
    for distance in range(1, 16):
        signal(z_neighbour(x, y, zl, zh, core, distance))
    signal(sibling)
    pl.semaphore_wait(pltpu.get_barrier_semaphore(), 31)

    def remote(src, dst, send, recv, device):
        return pltpu.make_async_remote_copy(
            src_ref=src, dst_ref=dst, send_sem=send, recv_sem=recv, device_id=device, device_id_type=MESH
        )

    set_x, set_y = set_of(x, y, zh, core)
    here = (set_x + 4 - x) % 4 == 0

    def to_owner(distance):
        there = (y + distance) % 4
        return remote(
            partial.at[:, there], plane_in.at[set_y], plane_send.at[distance], plane_recv.at[set_y],
            at(set_x, there, zl, zh, core),
        )

    def to_self():
        return pltpu.make_async_copy(partial.at[:, y], plane_in.at[set_y], plane_recv.at[set_y])

    for distance in (2, 1, 3):
        to_owner(distance).start()

    @pl.when(here)
    def _():
        to_self().start()

    @pl.when(jnp.logical_not(here))
    def _():
        to_owner(0).start()

    for member in range(4):
        remote(plane_in.at[member], plane_in.at[member], plane_send.at[0], plane_recv.at[member], sibling).wait_recv()

    def summed(part):
        result = plane_in[0, part].astype(F32)
        for member in range(1, 4):
            result += plane_in[member, part].astype(F32)
        return result

    z_out[...] = summed(1 - zh).astype(BF16)
    across = remote(z_out, z_in, z_sems.at[0], z_sems.at[1], z_neighbour(x, y, zl, zh, core, 8))
    across.start()
    own = summed(zh)
    across.wait_recv()
    mine = (own + z_in[...].astype(F32)).astype(BF16)
    agg[core] = mine
    agg_copy = remote(agg.at[core], agg.at[core], agg_sems.at[0], agg_sems.at[1], sibling)
    agg_copy.start()

    pre = jnp.dot(mine, weight[...], preferred_element_type=F32)
    sigma = jax.nn.sigmoid(pre)
    node_out[...] = (pre * sigma).astype(node_out.dtype)
    slope[core] = (cotangent[...].astype(F32) * sigma * (1.0 + pre * (1.0 - sigma))).astype(BF16)
    slope_copy = remote(slope.at[core], slope.at[core], slope_sems.at[0], slope_sems.at[1], sibling)
    slope_copy.start()
    agg_copy.wait_recv()
    slope_copy.wait_recv()

    columns = pl.ds(pl.multiple_of(core * 256, 256), 256)
    local = lax.dot_general(
        agg[:, :, columns].reshape(256, 256), slope[...].reshape(256, 512),
        (((0,), (0,)), ((), ())), preferred_element_type=F32,
    )
    grad[...] = local.reshape(16, 16, 512).astype(BF16)

    def grad_copy(distance):
        there = (spot + distance) % 16
        return remote(
            grad.at[there], grad_in.at[spot], grad_send.at[distance], grad_recv.at[spot], in_plane(distance)
        )

    for distance in range(1, 16):
        grad_copy(distance).start()
    rows_sum = grad[spot].astype(F32)
    for distance in range(1, 16):
        there = (spot + distance) % 16
        remote(grad_in.at[there], grad_in.at[there], grad_send.at[0], grad_recv.at[there], sibling).wait_recv()
        rows_sum += grad_in[there].astype(F32)
    for j in range(8):
        piece[j] = rows_sum[8 * (j // 4) : 8 * (j // 4) + 8, 128 * (j % 4) : 128 * (j % 4) + 128]

    def piece_copy(distance):
        there = (z + distance) % 16
        return remote(
            piece.at[there % 8], piece_in.at[z], piece_send.at[distance], piece_recv.at[z],
            z_neighbour(x, y, zl, zh, core, distance),
        )

    order = (8, 7, 9, 6, 10, 5, 11, 4, 12, 3, 13, 2, 14, 1, 15)
    for distance in order:
        piece_copy(distance).start()
    piece_in[z] = piece[zl]
    for distance in range(1, 16):
        there = (z + distance) % 16
        remote(piece_in.at[there], piece_in.at[there], piece_send.at[0], piece_recv.at[there], sibling).wait_recv()
    result = piece_in[0]
    for j in range(1, 16):
        result += piece_in[j]
    total[...] = result
    total_in[zl] = result

    def total_copy(distance):
        return remote(
            total, total_in.at[zl], total_send.at[distance + 3], total_recv.at[zl],
            z_neighbour(x, y, zl, zh, core, distance),
        )

    near = (4, -3, 3, -2, 2, -1, 1)
    for distance in near:
        total_copy(distance).start()
    for distance in range(1, 8):
        there = (zl + distance) % 8
        remote(total, total_in.at[there], total_send.at[0], total_recv.at[there], sibling).wait_recv()
    upper = jnp.concatenate([total_in[j] for j in range(4)], axis=1)
    lower = jnp.concatenate([total_in[j] for j in range(4, 8)], axis=1)
    whole[core, spot] = jnp.concatenate([upper, lower], axis=0).astype(BF16)

    def whole_copy(distance):
        return remote(
            whole.at[core, spot], whole.at[core, spot], whole_send.at[distance], whole_recv.at[spot],
            in_plane(distance),
        )

    for distance in range(1, 16):
        whole_copy(distance).start()
    for distance in range(1, 16):
        there = (spot + distance) % 16
        remote(
            whole.at[core, there], whole.at[core, there], whole_send.at[0], whole_recv.at[there], sibling
        ).wait_recv()
    final = remote(whole.at[core], whole.at[core], last_sems.at[0], last_sems.at[1], sibling)
    final.start()
    final.wait_recv()
    weight_grad[...] = whole[...].reshape(512, 512).astype(F32)

    for distance in (1, 2, 3):
        to_owner(distance).wait_send()

    @pl.when(jnp.logical_not(here))
    def _():
        to_owner(0).wait_send()

    across.wait_send()
    agg_copy.wait_send()
    slope_copy.wait_send()
    for distance in range(1, 16):
        grad_copy(distance).wait_send()
        piece_copy(distance).wait_send()
        whole_copy(distance).wait_send()
    for distance in near:
        total_copy(distance).wait_send()
    final.wait_send()


def finish(partial, weight, cotangent):
    sems = pltpu.SemaphoreType.DMA
    vmem = pl.BlockSpec(memory_space=pltpu.VMEM)
    return pl.pallas_call(
        finish_kernel,
        out_shape=(
            jax.ShapeDtypeStruct(cotangent.shape, BF16),
            jax.ShapeDtypeStruct(weight.shape, F32),
        ),
        in_specs=[vmem] * 3,
        out_specs=(vmem, vmem),
        scratch_shapes=[
            pltpu.VMEM((4, 2, 128, 512), BF16),
            pltpu.VMEM((128, 512), BF16),
            pltpu.VMEM((128, 512), BF16),
            pltpu.VMEM((2, 128, 512), BF16),
            pltpu.VMEM((2, 128, 512), BF16),
            pltpu.VMEM((16, 16, 512), BF16),
            pltpu.VMEM((16, 16, 512), BF16),
            pltpu.VMEM((8, 8, 128), F32),
            pltpu.VMEM((16, 8, 128), F32),
            pltpu.VMEM((8, 128), F32),
            pltpu.VMEM((8, 8, 128), F32),
            pltpu.VMEM((2, 16, 16, 512), BF16),
            sems((4,)),
            sems((4,)),
            sems((2,)),
            sems((2,)),
            sems((2,)),
            sems((16,)),
            sems((16,)),
            sems((16,)),
            sems((16,)),
            sems((8,)),
            sems((8,)),
            sems((16,)),
            sems((16,)),
            sems((2,)),
        ],
        compiler_params=pltpu.CompilerParams(
            collective_id=1, has_side_effects=True, vmem_limit_bytes=40 * 2**20
        ),
        name="finish",
    )(partial, weight, cotangent)


def tile_moves():
    moves = []
    for device in range(512):
        dom, rep = device // 8, device % 8
        x, y, zl, zh, core = (dom // 2) % 4, rep % 4, dom // 8, rep // 4, dom % 2
        host_x, host_y = hosted(x, y, zh, core)
        host = at(host_x, host_y, zl, zh, core)
        moves.append((device, host[0] * 8 + host[1]))
    return moves


def shards(features, tiles, tile_rows, tile_cols, tile_count, weight, cotangent):
    moves = tile_moves()
    axes = ("dom", "rep")
    slots = tile_rows.shape[0]
    numbers = lax.ppermute(jnp.concatenate([tile_rows, tile_cols, tile_count]), axes, moves)
    moved = lax.ppermute(tiles, axes, moves)
    blocks = gather(features)
    partial = tile_products(
        numbers[:slots], numbers[slots : 2 * slots], numbers[2 * slots :], moved, blocks.reshape(64, 128, 512)
    )
    return finish(partial.reshape(2, 4, 128, 512), weight, cotangent)


def solution(mesh):
    in_specs = (
        P("dom", None),
        P(("dom", "rep"), None, None),
        P(("dom", "rep")),
        P(("dom", "rep")),
        P(("dom", "rep")),
        P(),
        P(("dom", "rep"), None),
    )
    out_specs = (P(("dom", "rep"), None), P())
    return jax.shard_map(shards, mesh=mesh, in_specs=in_specs, out_specs=out_specs, check_vma=False)
```

```python
import types

import jax
import jax.numpy as jnp
from jax import lax
from jax.experimental import pallas as pl
from jax.experimental.pallas import tpu as pltpu
from jax.sharding import PartitionSpec as P

MESH = pl.DeviceIdType.MESH
BF16 = jnp.bfloat16
F32 = jnp.float32
I32 = jnp.int32

WIDTHS = (256, 128, 128)
UNITS = 2
SLOTS = 48
SLOT_STEP = 6


def at(x, y, zl, zh, core):
    return zl * 8 + x * 2 + core, zh * 4 + y


def hosted(x, y, zh, core):
    c = (2 * x + core + 16 - 4 * zh - y) % 8
    natural, natural_core = c // 2, c % 2
    b = (x + 8 - natural - 2 * zh) % 4
    host_x = (x + b + 3) % 4
    side = ((host_x + 4 - natural) % 4 - 1) // 2
    host_y = (1 - side) * (1 - natural_core) + side * (2 + natural_core)
    return host_x, host_y


def class_of(host_y):
    return host_y // 2, ((host_y + 1) // 2 + 1) % 2


def set_of(host_x, host_y, zh, core):
    side, natural_core = class_of(host_y)
    moved = (side + zh) % 2
    right = 1 - natural_core * (1 - core) * 2
    x = (host_x + 4 + moved * right) % 4
    low = (1 - natural_core) * core + natural_core * (1 - core) * 3
    high = (1 - natural_core) * (2 + core) + natural_core * (1 + core)
    return x, moved * low + (1 - moved) * high


def place():
    dom, rep = lax.axis_index("dom"), lax.axis_index("rep")
    return (dom // 2) % 4, rep % 4, dom // 8, rep // 4, dom % 2


def z_neighbour(x, y, zl, zh, core, distance):
    z = (zh * 8 + zl + distance + 16) % 16
    return at(x, y, z % 8, z // 8, core)


def signal(device):
    pl.semaphore_signal(pltpu.get_barrier_semaphore(), inc=1, device_id=device, device_id_type=MESH)


def remote(src, dst, send, recv, device):
    return pltpu.make_async_remote_copy(
        src_ref=src, dst_ref=dst, send_sem=send, recv_sem=recv, device_id=device, device_id_type=MESH
    )


def when_not(condition, action):
    pl.when(jnp.logical_not(condition))(action)


def sort_slots(rows, cols, count, numbers):
    shape = (SLOTS, SLOTS)
    sub = lax.broadcasted_iota(I32, shape, 0).astype(F32)
    lane = lax.broadcasted_iota(I32, shape, 1).astype(F32)
    eye = (sub == lane).astype(F32)

    def column(row):
        return jnp.sum(eye * row, axis=1, keepdims=True)

    live = lane[:1] < count[...].reshape(1, 1).astype(F32)
    key = jnp.where(live, rows[...].reshape(1, SLOTS).astype(F32), 8.0)
    col = cols[...].reshape(1, SLOTS)
    block = ((col >> 6) * 8 + (col & 7)).astype(F32)
    unique = key * 64.0 + lane[:1]
    key_column = column(key)
    rank = jnp.sum((unique < column(unique)).astype(F32), axis=1, keepdims=True)
    chosen = (rank == lane).astype(F32)
    after = (rank + 1.0 == lane).astype(F32)
    sorted_key = jnp.sum(chosen * key_column, axis=0, keepdims=True)
    key_before = jnp.sum(after * key_column, axis=0, keepdims=True)
    numbers[0:1, 0:SLOTS] = jnp.sum(chosen * sub, axis=0, keepdims=True).astype(I32)
    numbers[1:2, 0:SLOTS] = jnp.sum(chosen * column(block), axis=0, keepdims=True).astype(I32)
    numbers[2:3, 0:SLOTS] = (sorted_key == key_before).astype(I32)
    ends = jnp.where(key_column == lane, rank + 1.0, 0.0)
    numbers[3:4, 0:SLOTS] = jnp.max(ends, axis=0, keepdims=True).astype(I32)


def scratch():
    vmem, sems = pltpu.VMEM, pltpu.SemaphoreType.DMA
    chunks = len(WIDTHS)
    names = {
        "numbers": vmem((8, 128), I32),
        "numbers_in": vmem((8, 128), I32),
        "table": pltpu.SMEM((8, 128), I32),
        "tile_set": vmem((SLOTS, 128, 128), BF16),
        "products": vmem((SLOTS + 1, 128, max(WIDTHS)), F32),
        "weight": vmem((512, 512), BF16),
        "cotangent": vmem((128, 512), BF16),
        "load_sems": sems((2,)),
        "agg": vmem((2, 128, 512), BF16),
        "slope": vmem((2, 128, 512), BF16),
        "grad": vmem((16, 16, 512), BF16),
        "grad_in": vmem((16, 16, 512), BF16),
        "piece": vmem((8, 8, 128), F32),
        "piece_in": vmem((16, 8, 128), F32),
        "total": vmem((8, 128), F32),
        "total_in": vmem((8, 8, 128), F32),
        "whole": vmem((2, 16, 16, 512), BF16),
        "set_sems": sems((5,)),
        "own_send": sems((chunks, UNITS, 2)),
        "own_recv": sems((chunks, UNITS)),
        "ring_send": sems((chunks, 2, 4, UNITS)),
        "ring_recv": sems((chunks, 2, 4, UNITS)),
        "pair_send": sems((chunks, 8, UNITS)),
        "pair_recv": sems((chunks, 8, UNITS)),
        "plane_send": sems((chunks, 4)),
        "plane_recv": sems((chunks, 4)),
        "z_send": sems((chunks,)),
        "z_recv": sems((chunks,)),
        "agg_send": sems((chunks,)),
        "agg_recv": sems((chunks,)),
        "slope_sems": sems((2,)),
        "grad_send": sems((16,)),
        "grad_recv": sems((16,)),
        "piece_send": sems((16,)),
        "piece_recv": sems((16,)),
        "total_send": sems((8,)),
        "total_recv": sems((8,)),
        "whole_send": sems((16,)),
        "whole_recv": sems((16,)),
        "last_sems": sems((2,)),
    }
    for q, width in enumerate(WIDTHS):
        names["blocks%d" % q] = vmem((64, 128, width), BF16)
        names["partial%d" % q] = vmem((2, 4, 128, width), BF16)
        names["plane_in%d" % q] = vmem((4, 2, 128, width), BF16)
        names["z_out%d" % q] = vmem((128, width), BF16)
        names["z_in%d" % q] = vmem((128, width), BF16)
        names["own%d" % q] = vmem((128, width), F32)
    return names


def layer_kernel(features, tiles, rows, cols, count, weight_in, cotangent_in, node_out, weight_grad, *refs):
    s = types.SimpleNamespace(**dict(zip(scratch(), refs)))
    chunks = len(WIDTHS)
    starts = [sum(WIDTHS[:q]) for q in range(chunks)]

    def of(name, q):
        return getattr(s, name + str(q))

    x, y, zl, zh, core = place()
    z = zh * 8 + zl
    spot = x * 4 + y
    sibling = at(x, y, zl, zh, 1 - core)
    up = z_neighbour(x, y, zl, zh, core, 1)
    down = z_neighbour(x, y, zl, zh, core, -1)
    side, natural_core = class_of(y)
    is_source = core == natural_core
    source = at((x + 3 + 2 * side) % 4, y, zl, zh, natural_core)
    target_x = (x + 1 + 2 * side) % 4

    def in_plane(distance):
        there = (spot + distance) % 16
        return at(there // 4, there % 4, zl, zh, core)

    weight, cotangent = s.weight, s.cotangent
    loads = [
        pltpu.make_async_copy(weight_in, weight, s.load_sems.at[0]),
        pltpu.make_async_copy(cotangent_in, cotangent, s.load_sems.at[1]),
    ]
    for load in loads:
        load.start()

    signal(up)
    signal(down)
    signal(sibling)
    when_not(is_source, lambda: signal(source))
    for distance in (8, 7, 9, 6, 10, 5, 11, 4, 12, 3, 13, 2, 14):
        signal(z_neighbour(x, y, zl, zh, core, distance))
    for distance in range(1, 16):
        signal(in_plane(distance))
    sort_slots(rows, cols, count, s.numbers)
    s.products[0] = jnp.zeros(s.products.shape[1:], F32)
    pl.semaphore_wait(pltpu.get_barrier_semaphore(), 31 + (1 - (core + natural_core) % 2))

    def block_part(q, distance, h, of_core):
        size = 4 // UNITS
        return of("blocks", q).at[pl.ds((zl + distance + 8) % 8 * 8 + of_core * 4 + h * size, size)]

    def own_copy(q, h, to_core):
        size = 4 // UNITS
        return remote(
            features.at[pl.ds(to_core * 4 + h * size, size), :, pl.ds(starts[q], WIDTHS[q])],
            block_part(q, 0, h, to_core), s.own_send.at[q, h, to_core], s.own_recv.at[q, h],
            at(target_x, y, zl, zh, to_core),
        )

    def send_own(q):
        @pl.when(is_source)
        def _():
            for h in range(UNITS):
                for to_core in range(2):
                    own_copy(q, h, to_core).start()

    def hop(q, step, h, upward):
        ref = block_part(q, -step if upward else step, h, core)
        way = 0 if upward else 1
        return remote(
            ref, ref, s.ring_send.at[q, way, step, h], s.ring_recv.at[q, way, step, h], up if upward else down
        )

    def arrival(q, step, h, upward):
        ref = block_part(q, -step - 1 if upward else step + 1, h, core)
        way = 0 if upward else 1
        return remote(ref, ref, s.ring_send.at[q, way, step, h], s.ring_recv.at[q, way, step, h], sibling)

    def pair_copy(q, distance, h, of_core):
        ref = block_part(q, distance, h, of_core)
        return remote(ref, ref, s.pair_send.at[q, distance + 4, h], s.pair_recv.at[q, distance + 4, h], sibling)

    def hops(h, upward):
        return 4 if (h < UNITS // 2) == upward else 3

    def own_event(q, h):
        own_copy(q, h, 0).wait_recv()
        hop(q, 0, h, True).start()
        hop(q, 0, h, False).start()
        pair_copy(q, 0, h, core).start()

    def ring_event(q, step, h, upward):
        arrival(q, step, h, upward).wait_recv()
        if step + 1 < hops(h, upward):
            hop(q, step + 1, h, upward).start()
        distance = -step - 1 if upward or step == 3 else step + 1
        pair_copy(q, distance, h, core).start()

    def ring_events(q, steps):
        return [
            lambda step=step, h=h, upward=upward: ring_event(q, step, h, upward)
            for step in steps
            for h in range(UNITS)
            for upward in (True, False)
            if step < hops(h, upward)
        ]

    def own_events(q):
        return [lambda h=h: own_event(q, h) for h in range(UNITS)]

    def pair_arrivals(q):
        for distance in (0, -1, 1, -2, 2, -3, 3, -4):
            for h in range(UNITS):
                pair_copy(q, distance, h, 1 - core).wait_recv()

    host_x, host_y = hosted(x, y, zh, core)
    stays = (host_x + 4 - x) % 4 + (host_y + 4 - y) % 4 == 0
    host = at(host_x, host_y, zl, zh, core)
    set_copies = [
        remote(s.numbers, s.numbers_in, s.set_sems.at[0], s.set_sems.at[1], host),
        remote(tiles, s.tile_set, s.set_sems.at[2], s.set_sems.at[3], host),
    ]
    local_copies = [
        pltpu.make_async_copy(s.numbers, s.numbers_in, s.set_sems.at[1]),
        pltpu.make_async_copy(tiles, s.tile_set, s.set_sems.at[3]),
    ]

    def send_set():
        @pl.when(stays)
        def _():
            for copy in local_copies:
                copy.start()

        @pl.when(jnp.logical_not(stays))
        def _():
            for copy in set_copies:
                copy.start()

    def receive_set():
        for copy in set_copies:
            copy.wait_recv()
        to_table = pltpu.make_async_copy(s.numbers_in, s.table, s.set_sems.at[4])
        to_table.start()
        to_table.wait()

    def entry(row, place, top):
        return jnp.minimum(jnp.maximum(s.table[row, place], 0), top)

    def multiply(q, first):
        width = WIDTHS[q]

        def one(j, carry):
            tile = s.tile_set[entry(0, j, SLOTS - 1)]
            product = jnp.dot(tile, of("blocks", q)[entry(1, j, 63)], preferred_element_type=F32)
            same = s.table[2, j].astype(F32)
            s.products[j + 1, :, 0:width] = product + same * s.products[j, :, 0:width]
            return carry

        lax.fori_loop(first, first + SLOT_STEP, one, 0)

    def multiplies(q):
        return [lambda first=first: multiply(q, first) for first in range(0, SLOTS, SLOT_STEP)]

    set_x, set_y = set_of(x, y, zh, core)
    here = (set_x + 4 - x) % 4 == 0

    def to_owner(q, distance):
        there = (y + distance) % 4
        return remote(
            of("partial", q).at[:, there], of("plane_in", q).at[set_y], s.plane_send.at[q, distance],
            s.plane_recv.at[q, set_y], at(set_x, there, zl, zh, core),
        )

    def send_partial(q):
        width = WIDTHS[q]
        for t in range(8):
            of("partial", q)[t // 4, t % 4] = s.products[entry(3, t, SLOTS), :, 0:width].astype(BF16)
        for distance in (2, 1, 3):
            to_owner(q, distance).start()

        @pl.when(here)
        def _():
            pltpu.make_async_copy(
                of("partial", q).at[:, y], of("plane_in", q).at[set_y], s.plane_recv.at[q, set_y]
            ).start()

        when_not(here, lambda: to_owner(q, 0).start())

    def across(q):
        return remote(
            of("z_out", q), of("z_in", q), s.z_send.at[q], s.z_recv.at[q], z_neighbour(x, y, zl, zh, core, 8)
        )

    def sum_plane(q):
        for member in range(4):
            ref = of("plane_in", q).at[member]
            remote(ref, ref, s.plane_send.at[q, 0], s.plane_recv.at[q, member], sibling).wait_recv()

        def summed(part):
            result = of("plane_in", q)[0, part].astype(F32)
            for member in range(1, 4):
                result += of("plane_in", q)[member, part].astype(F32)
            return result

        of("z_out", q)[...] = summed(1 - zh).astype(BF16)
        across(q).start()
        of("own", q)[...] = summed(zh)

    def agg_copy(q, of_core):
        ref = s.agg.at[of_core, :, pl.ds(starts[q], WIDTHS[q])]
        return remote(ref, ref, s.agg_send.at[q], s.agg_recv.at[q], sibling)

    def aggregate(q):
        across(q).wait_recv()
        mine = (of("own", q)[...] + of("z_in", q)[...].astype(F32)).astype(BF16)
        s.agg[core, :, starts[q] : starts[q] + WIDTHS[q]] = mine
        agg_copy(q, core).start()
        return jnp.dot(mine, weight[starts[q] : starts[q] + WIDTHS[q], :], preferred_element_type=F32)

    events = []
    for slot in range(2 * chunks + 3):
        for q in range(chunks):
            step = slot - 2 * q - 1
            if step == -1:
                events += [(q, step, event) for event in own_events(q)]
            elif 0 <= step < 4:
                events += [(q, step, event) for event in ring_events(q, [step])]

    send_own(0)
    send_set()
    for q in range(1, chunks):
        send_own(q)
    work, waiting = [], list(range(chunks - 1))
    for place_in_list, (q, step, event) in enumerate(events):
        event()
        for _ in range(2):
            if work:
                work.pop(0)()
        left = [later[:2] for later in events[place_in_list + 1 :]]
        started = step >= 2 and q > 0 and (q, step) not in left
        if waiting and waiting[0] not in [later for later, _ in left] and (started or waiting[0] > 0):
            ready = waiting.pop(0)
            work.append(lambda ready=ready: pair_arrivals(ready))
            if ready == 0:
                work.append(receive_set)
            work += multiplies(ready) + [lambda ready=ready: send_partial(ready)]
    for item in work:
        item()
    for q in range(chunks - 2):
        sum_plane(q)
    pair_arrivals(chunks - 1)
    for item in multiplies(chunks - 1):
        item()
    send_partial(chunks - 1)
    sum_plane(chunks - 2)
    for load in loads:
        load.wait()
    pre = aggregate(0)
    for q in range(1, chunks - 1):
        pre += aggregate(q)
    sum_plane(chunks - 1)
    pre += aggregate(chunks - 1)

    sigma = jax.nn.sigmoid(pre)
    s.slope[core] = (cotangent[...].astype(F32) * sigma * (1.0 + pre * (1.0 - sigma))).astype(BF16)
    slope_copy = remote(s.slope.at[core], s.slope.at[core], s.slope_sems.at[0], s.slope_sems.at[1], sibling)
    slope_copy.start()
    node_out[...] = (pre * sigma).astype(node_out.dtype)
    for q in range(chunks):
        agg_copy(q, 1 - core).wait_recv()
    slope_copy.wait_recv()

    columns = pl.ds(pl.multiple_of(core * 256, 256), 256)
    local = lax.dot_general(
        s.agg[:, :, columns].reshape(256, 256), s.slope[...].reshape(256, 512),
        (((0,), (0,)), ((), ())), preferred_element_type=F32,
    )
    s.grad[...] = local.reshape(16, 16, 512).astype(BF16)

    def grad_copy(distance):
        there = (spot + distance) % 16
        return remote(
            s.grad.at[there], s.grad_in.at[spot], s.grad_send.at[distance], s.grad_recv.at[spot], in_plane(distance)
        )

    for distance in range(1, 16):
        grad_copy(distance).start()
    rows_sum = s.grad[spot].astype(F32)
    for distance in range(1, 16):
        there = (spot + distance) % 16
        ref = s.grad_in.at[there]
        remote(ref, ref, s.grad_send.at[0], s.grad_recv.at[there], sibling).wait_recv()
        rows_sum += s.grad_in[there].astype(F32)
    for j in range(8):
        s.piece[j] = rows_sum[8 * (j // 4) : 8 * (j // 4) + 8, 128 * (j % 4) : 128 * (j % 4) + 128]

    def piece_copy(distance):
        there = (z + distance) % 16
        return remote(
            s.piece.at[there % 8], s.piece_in.at[z], s.piece_send.at[distance], s.piece_recv.at[z],
            z_neighbour(x, y, zl, zh, core, distance),
        )

    for distance in (8, 7, 9, 6, 10, 5, 11, 4, 12, 3, 13, 2, 14, 1, 15):
        piece_copy(distance).start()
    s.piece_in[z] = s.piece[zl]
    for distance in range(1, 16):
        there = (z + distance) % 16
        ref = s.piece_in.at[there]
        remote(ref, ref, s.piece_send.at[0], s.piece_recv.at[there], sibling).wait_recv()
    result = s.piece_in[0]
    for j in range(1, 16):
        result += s.piece_in[j]
    s.total[...] = result
    s.total_in[zl] = result

    def total_copy(distance):
        return remote(
            s.total, s.total_in.at[zl], s.total_send.at[distance + 3], s.total_recv.at[zl],
            z_neighbour(x, y, zl, zh, core, distance),
        )

    near = (4, -3, 3, -2, 2, -1, 1)
    for distance in near:
        total_copy(distance).start()
    for distance in range(1, 8):
        there = (zl + distance) % 8
        remote(s.total, s.total_in.at[there], s.total_send.at[0], s.total_recv.at[there], sibling).wait_recv()
    upper = jnp.concatenate([s.total_in[j] for j in range(4)], axis=1)
    lower = jnp.concatenate([s.total_in[j] for j in range(4, 8)], axis=1)
    s.whole[core, spot] = jnp.concatenate([upper, lower], axis=0).astype(BF16)

    def whole_copy(distance):
        ref = s.whole.at[core, spot]
        return remote(ref, ref, s.whole_send.at[distance], s.whole_recv.at[spot], in_plane(distance))

    for distance in range(1, 16):
        whole_copy(distance).start()
    for distance in range(1, 16):
        there = (spot + distance) % 16
        ref = s.whole.at[core, there]
        remote(ref, ref, s.whole_send.at[0], s.whole_recv.at[there], sibling).wait_recv()
    final = remote(s.whole.at[core], s.whole.at[core], s.last_sems.at[0], s.last_sems.at[1], sibling)
    final.start()
    final.wait_recv()
    weight_grad[...] = s.whole[...].reshape(512, 512).astype(F32)

    for q in range(chunks):
        @pl.when(is_source)
        def _():
            for h in range(UNITS):
                for to_core in range(2):
                    own_copy(q, h, to_core).wait_send()

        for h in range(UNITS):
            for upward in (True, False):
                for step in range(hops(h, upward)):
                    hop(q, step, h, upward).wait_send()
            for distance in range(-4, 4):
                pair_copy(q, distance, h, core).wait_send()
        for distance in (1, 2, 3):
            to_owner(q, distance).wait_send()
        when_not(here, lambda: to_owner(q, 0).wait_send())
        across(q).wait_send()
        agg_copy(q, core).wait_send()

    @pl.when(jnp.logical_not(stays))
    def _():
        for copy in set_copies:
            copy.wait_send()

    slope_copy.wait_send()
    for distance in range(1, 16):
        grad_copy(distance).wait_send()
        piece_copy(distance).wait_send()
        whole_copy(distance).wait_send()
    for distance in near:
        total_copy(distance).wait_send()
    final.wait_send()


def shards(features, tiles, tile_rows, tile_cols, tile_count, weight, cotangent):
    vmem = pl.BlockSpec(memory_space=pltpu.VMEM)
    anywhere = pl.BlockSpec(memory_space=pl.ANY)
    return pl.pallas_call(
        layer_kernel,
        out_shape=(
            jax.ShapeDtypeStruct(cotangent.shape, BF16),
            jax.ShapeDtypeStruct(weight.shape, F32),
        ),
        in_specs=[anywhere, anywhere, vmem, vmem, vmem, anywhere, anywhere],
        out_specs=(vmem, vmem),
        scratch_shapes=list(scratch().values()),
        compiler_params=pltpu.CompilerParams(
            collective_id=0, has_side_effects=True, vmem_limit_bytes=60 * 2**20
        ),
        name="layer",
    )(
        features.reshape(8, 128, 512), tiles, tile_rows, tile_cols, tile_count, weight, cotangent,
    )


def solution(mesh):
    in_specs = (
        P("dom", None),
        P(("dom", "rep"), None, None),
        P(("dom", "rep")),
        P(("dom", "rep")),
        P(("dom", "rep")),
        P(),
        P(("dom", "rep"), None),
    )
    out_specs = (P(("dom", "rep"), None), P())
    return jax.shard_map(shards, mesh=mesh, in_specs=in_specs, out_specs=out_specs, check_vma=False)
```

```python
import types

import jax
import jax.numpy as jnp
from jax import lax
from jax.experimental import pallas as pl
from jax.experimental.pallas import tpu as pltpu
from jax.sharding import PartitionSpec as P

MESH = pl.DeviceIdType.MESH
BF16 = jnp.bfloat16
F32 = jnp.float32
I32 = jnp.int32

WIDTHS = (256, 256)
ALONE, BOTH, FROM_Y = range(3)
SLOTS = 48
PIECES = 3
SLOT_STEP = 8
FAR_FIRST = sorted(
    [(dx, dy) for dx in range(4) for dy in range(4) if dx or dy],
    key=lambda d: -min(d[0], 4 - d[0]) - min(d[1], 4 - d[1]),
)


def at(x, y, zl, zh, core):
    return zl * 8 + x * 2 + core, zh * 4 + y


def hosted(x, y, zh, core):
    c = (2 * x + core + 16 - 4 * zh - y) % 8
    member = ((y + 1) // 2) % 2
    return c // 2, (1 - c % 2) * member + (c % 2) * (3 - member)


def set_of(host_x, host_y, zh, core):
    natural_core = host_y // 2
    member = (1 - natural_core) * host_y + natural_core * (3 - host_y)
    other = (core + natural_core) % 2
    y = (1 - other) * 2 * member + other * (3 - 2 * member)
    return ((2 * host_x + natural_core + 4 * zh + y - core) // 2) % 4, y


def place():
    dom, rep = lax.axis_index("dom"), lax.axis_index("rep")
    return (dom // 2) % 4, rep % 4, dom // 8, rep // 4, dom % 2


def z_neighbour(x, y, zl, zh, core, distance):
    z = (zh * 8 + zl + distance + 16) % 16
    return at(x, y, z % 8, z // 8, core)


def signal(device):
    pl.semaphore_signal(pltpu.get_barrier_semaphore(), inc=1, device_id=device, device_id_type=MESH)


def remote(src, dst, send, recv, device):
    return pltpu.make_async_remote_copy(
        src_ref=src, dst_ref=dst, send_sem=send, recv_sem=recv, device_id=device, device_id_type=MESH
    )


def when_not(condition, action):
    pl.when(jnp.logical_not(condition))(action)


def sort_slots(rows, cols, count, numbers):
    shape = (SLOTS, SLOTS)
    sub = lax.broadcasted_iota(I32, shape, 0).astype(F32)
    lane = lax.broadcasted_iota(I32, shape, 1).astype(F32)
    eye = (sub == lane).astype(F32)

    def column(row):
        return jnp.sum(eye * row, axis=1, keepdims=True)

    live = lane[:1] < count[...].reshape(1, 1).astype(F32)
    key = jnp.where(live, rows[...].reshape(1, SLOTS).astype(F32), 8.0)
    col = cols[...].reshape(1, SLOTS)
    block = ((col >> 6) * 8 + (col & 7)).astype(F32)
    unique = key * 64.0 + lane[:1]
    key_column = column(key)
    rank = jnp.sum((unique < column(unique)).astype(F32), axis=1, keepdims=True)
    chosen = (rank == lane).astype(F32)
    after = (rank + 1.0 == lane).astype(F32)
    sorted_key = jnp.sum(chosen * key_column, axis=0, keepdims=True)
    key_before = jnp.sum(after * key_column, axis=0, keepdims=True)
    numbers[0:1, 0:SLOTS] = jnp.sum(chosen * sub, axis=0, keepdims=True).astype(I32)
    numbers[1:2, 0:SLOTS] = jnp.sum(chosen * column(block), axis=0, keepdims=True).astype(I32)
    numbers[2:3, 0:SLOTS] = (sorted_key == key_before).astype(I32)
    ends = jnp.where(key_column == lane, rank + 1.0, 0.0)
    numbers[3:4, 0:SLOTS] = jnp.max(ends, axis=0, keepdims=True).astype(I32)


def scratch():
    vmem, sems = pltpu.VMEM, pltpu.SemaphoreType.DMA
    chunks = len(WIDTHS)
    names = {
        "numbers": vmem((8, 128), I32),
        "numbers_in": vmem((8, 128), I32),
        "own_table": pltpu.SMEM((8, 128), I32),
        "table": pltpu.SMEM((8, 128), I32),
        "tiles": vmem((SLOTS, 128, 128), BF16),
        "sorted_tiles": vmem((SLOTS, 128, 128), BF16),
        "tile_set": vmem((SLOTS, 128, 128), BF16),
        "weight": vmem((512, 512), BF16),
        "cotangent": vmem((128, 512), BF16),
        "load_sems": sems((2,)),
        "agg": vmem((2, 128, 512), BF16),
        "slope": vmem((2, 128, 512), BF16),
        "grad": vmem((16, 16, 512), BF16),
        "grad_in": vmem((16, 16, 512), BF16),
        "piece": vmem((8, 8, 128), F32),
        "piece_in": vmem((16, 8, 128), F32),
        "total": vmem((8, 128), F32),
        "total_in": vmem((8, 8, 128), F32),
        "whole": vmem((2, 16, 16, 512), BF16),
        "set_send": sems((PIECES + 1,)),
        "set_recv": sems((PIECES + 1,)),
        "local_sems": sems((3,)),
        "own_send": sems((chunks, 2)),
        "own_recv": sems((chunks, 2)),
        "ring_send": sems((chunks, 2, 4, 2)),
        "ring_recv": sems((chunks, 2, 4, 2)),
        "y_send": sems((chunks, 8)),
        "y_recv": sems((chunks, 8)),
        "pair_send": sems((chunks, 8, 3)),
        "pair_recv": sems((chunks, 8, 3)),
        "plane_send": sems((chunks, 4)),
        "plane_recv": sems((chunks, 4)),
        "z_send": sems((chunks,)),
        "z_recv": sems((chunks,)),
        "agg_send": sems((chunks,)),
        "agg_recv": sems((chunks,)),
        "slope_sems": sems((2,)),
        "grad_send": sems((16,)),
        "grad_recv": sems((16,)),
        "piece_send": sems((16,)),
        "piece_recv": sems((16,)),
        "total_send": sems((8,)),
        "total_recv": sems((8,)),
        "whole_send": sems((16,)),
        "whole_recv": sems((16,)),
        "last_sems": sems((2,)),
    }
    for q, width in enumerate(WIDTHS):
        names["blocks%d" % q] = vmem((64, 128, width), BF16)
        names["products%d" % q] = vmem((SLOTS + 1, 128, width), F32)
        names["partial%d" % q] = vmem((2, 4, 128, width), BF16)
        names["plane_in%d" % q] = vmem((4, 2, 128, width), BF16)
        names["z_out%d" % q] = vmem((128, width), BF16)
        names["z_in%d" % q] = vmem((128, width), BF16)
        names["own%d" % q] = vmem((128, width), F32)
    return names


def layer_kernel(features, tiles_in, rows, cols, count, weight_in, cotangent_in, node_out, weight_grad, *refs):
    s = types.SimpleNamespace(**dict(zip(scratch(), refs)))
    chunks = len(WIDTHS)
    starts = [sum(WIDTHS[:q]) for q in range(chunks)]

    def of(name, q):
        return getattr(s, name + str(q))

    x, y, zl, zh, core = place()
    z = zh * 8 + zl
    spot = x * 4 + y
    sibling = at(x, y, zl, zh, 1 - core)
    up = z_neighbour(x, y, zl, zh, core, 1)
    down = z_neighbour(x, y, zl, zh, core, -1)
    natural_core = y // 2
    is_source = core == natural_core
    member = y % 2
    y_pair = at(x, y + 1 - 2 * member, zl, zh, core)

    def in_plane(step):
        return at((x + step[0]) % 4, (y + step[1]) % 4, zl, zh, core)

    def spot_at(step):
        return (x + step[0]) % 4 * 4 + (y + step[1]) % 4

    weight, cotangent = s.weight, s.cotangent
    loads = [
        pltpu.make_async_copy(weight_in, weight, s.load_sems.at[0]),
        pltpu.make_async_copy(cotangent_in, cotangent, s.load_sems.at[1]),
    ]
    load_tiles = pltpu.make_async_copy(tiles_in, s.tiles, s.local_sems.at[0])
    load_tiles.start()

    signal(up)
    signal(down)
    signal(sibling)
    for distance in (8, 7, 9, 6, 10, 5, 11, 4, 12, 3, 13, 2, 14):
        signal(z_neighbour(x, y, zl, zh, core, distance))
    for step in FAR_FIRST:
        signal(in_plane(step))
    sort_slots(rows, cols, count, s.numbers)
    to_own_table = pltpu.make_async_copy(s.numbers, s.own_table, s.local_sems.at[1])
    to_own_table.start()
    for q in range(chunks):
        of("products", q)[0] = jnp.zeros((128, WIDTHS[q]), F32)
    load_tiles.wait()
    to_own_table.wait()
    for load in loads:
        load.start()

    def entry(table, row, place, top):
        return jnp.minimum(jnp.maximum(table[row, place], 0), top)

    def place_tile(j, carry):
        s.sorted_tiles[j] = s.tiles[entry(s.own_table, 0, j, SLOTS - 1)]
        return carry

    lax.fori_loop(0, SLOTS, place_tile, 0, unroll=2)
    pl.semaphore_wait(pltpu.get_barrier_semaphore(), 31)

    def block_rows(distance, of_core):
        return (zl + distance + 8) % 8 * 8 + of_core * 4

    def block_part(q, distance, unit, of_core):
        row = block_rows(distance, of_core)
        row = row + (member if unit == ALONE else 2 if unit == BOTH else 1 - member)
        return of("blocks", q).at[pl.ds(row, 2 if unit == BOTH else 1)]

    def own_part(q, of_core):
        columns = pl.ds(starts[q], WIDTHS[q])
        return features.at[pl.ds(of_core * 4, 4), :, columns], of("blocks", q).at[pl.ds(block_rows(0, of_core), 4)]

    def own_local(q, of_core):
        return pltpu.make_async_copy(*own_part(q, of_core), s.own_recv.at[q, of_core])

    def own_remote(q, of_core):
        return remote(*own_part(q, of_core), s.own_send.at[q, of_core], s.own_recv.at[q, of_core], sibling)

    def send_own(q):
        @pl.when(is_source)
        def _():
            own_remote(q, 1 - core).start()
            own_local(q, core).start()
            own_remote(q, core).start()
            own_local(q, 1 - core).start()

    def hop(q, step, unit, upward):
        ref = block_part(q, -step if upward else step, unit, core)
        way = 0 if upward else 1
        return remote(
            ref, ref, s.ring_send.at[q, way, step, unit], s.ring_recv.at[q, way, step, unit], up if upward else down
        )

    def arrival(q, step, unit, upward):
        ref = block_part(q, -step - 1 if upward else step + 1, unit, core)
        way = 0 if upward else 1
        return remote(ref, ref, s.ring_send.at[q, way, step, unit], s.ring_recv.at[q, way, step, unit], sibling)

    def y_copy(q, distance, unit):
        ref = block_part(q, distance, unit, core)
        return remote(ref, ref, s.y_send.at[q, distance + 4], s.y_recv.at[q, distance + 4], y_pair)

    def pair_copy(q, distance, unit, of_core):
        ref = block_part(q, distance, unit, of_core)
        return remote(ref, ref, s.pair_send.at[q, distance + 4, unit], s.pair_recv.at[q, distance + 4, unit], sibling)

    def hops(q, unit, upward):
        return 4 if (unit == (ALONE if q % 2 == 0 else BOTH)) == upward else 3

    def own_event(q):
        own_local(q, core).wait()
        for unit in (ALONE, BOTH):
            hop(q, 0, unit, True).start()
            hop(q, 0, unit, False).start()

    def ring_event(q, step, unit, upward):
        arrival(q, step, unit, upward).wait_recv()
        if step + 1 < hops(q, unit, upward):
            hop(q, step + 1, unit, upward).start()
        distance = -step - 1 if upward or step == 3 else step + 1
        if unit == ALONE:
            y_copy(q, distance, ALONE).start()
        pair_copy(q, distance, unit, core).start()

    def y_event(q, distance):
        y_copy(q, distance, FROM_Y).wait_recv()
        pair_copy(q, distance, FROM_Y, core).start()

    def ring_events(q, step):
        return [
            lambda unit=unit, upward=upward: ring_event(q, step, unit, upward)
            for unit in (ALONE, BOTH)
            for upward in (True, False)
            if step < hops(q, unit, upward)
        ]

    def y_events(q, step):
        distances = (-4,) if step == 3 else (-step - 1, step + 1)
        return [lambda distance=distance: y_event(q, distance) for distance in distances]

    def pair_arrivals(q):
        own_local(q, 1 - core).wait()
        for distance in (-1, 1, -2, 2, -3, 3, -4):
            for unit in (ALONE, BOTH, FROM_Y):
                pair_copy(q, distance, unit, 1 - core).wait_recv()

    host_x, host_y = hosted(x, y, zh, core)
    stays = (host_x + 4 - x) % 4 + (host_y + 4 - y) % 4 == 0
    host = at(host_x, host_y, zl, zh, core)
    per_piece = SLOTS // PIECES
    set_parts = [(s.numbers, s.numbers_in)] + [
        (s.sorted_tiles.at[pl.ds(i * per_piece, per_piece)], s.tile_set.at[pl.ds(i * per_piece, per_piece)])
        for i in range(PIECES)
    ]

    def set_remote(i):
        return remote(*set_parts[i], s.set_send.at[i], s.set_recv.at[i], host)

    def set_local(i):
        return pltpu.make_async_copy(*set_parts[i], s.set_recv.at[i])

    def send_set():
        @pl.when(stays)
        def _():
            for i in range(PIECES + 1):
                set_local(i).start()

        @pl.when(jnp.logical_not(stays))
        def _():
            for i in range(PIECES + 1):
                set_remote(i).start()

    def receive_table():
        set_local(0).wait()
        to_table = pltpu.make_async_copy(s.numbers_in, s.table, s.local_sems.at[2])
        to_table.start()
        to_table.wait()

    def receive_piece(i):
        set_local(i + 1).wait()

    def multiply(q, first):
        def four(i, carry):
            base = first + 4 * i
            total = of("products", q)[base]
            for j in range(4):
                block = of("blocks", q)[entry(s.table, 1, base + j, 63)]
                product = jnp.dot(s.tile_set[base + j], block, preferred_element_type=F32)
                total = product + s.table[2, base + j].astype(F32) * total
                of("products", q)[base + j + 1] = total
            return carry

        lax.fori_loop(0, SLOT_STEP // 4, four, 0)

    def multiplies(q, pieces):
        slots = range(pieces[0] * per_piece, (pieces[-1] + 1) * per_piece, SLOT_STEP)
        return [lambda first=first: multiply(q, first) for first in slots]

    set_x, set_y = set_of(x, y, zh, core)
    here = (set_x + 4 - x) % 4 == 0

    def to_owner(q, distance):
        there = (y + distance) % 4
        return remote(
            of("partial", q).at[:, there], of("plane_in", q).at[set_y], s.plane_send.at[q, distance],
            s.plane_recv.at[q, set_y], at(set_x, there, zl, zh, core),
        )

    def send_partial(q):
        for t in range(8):
            of("partial", q)[t // 4, t % 4] = of("products", q)[entry(s.table, 3, t, SLOTS)].astype(BF16)
        for distance in (2, 1, 3):
            to_owner(q, distance).start()

        @pl.when(here)
        def _():
            pltpu.make_async_copy(
                of("partial", q).at[:, y], of("plane_in", q).at[set_y], s.plane_recv.at[q, set_y]
            ).start()

        when_not(here, lambda: to_owner(q, 0).start())

    def across(q):
        return remote(
            of("z_out", q), of("z_in", q), s.z_send.at[q], s.z_recv.at[q], z_neighbour(x, y, zl, zh, core, 8)
        )

    def sum_plane(q):
        for member in range(4):
            ref = of("plane_in", q).at[member]
            remote(ref, ref, s.plane_send.at[q, 0], s.plane_recv.at[q, member], sibling).wait_recv()

        def summed(part):
            result = of("plane_in", q)[0, part].astype(F32)
            for member in range(1, 4):
                result += of("plane_in", q)[member, part].astype(F32)
            return result

        of("z_out", q)[...] = summed(1 - zh).astype(BF16)
        across(q).start()
        of("own", q)[...] = summed(zh)

    def agg_copy(q, of_core):
        ref = s.agg.at[of_core, :, pl.ds(starts[q], WIDTHS[q])]
        return remote(ref, ref, s.agg_send.at[q], s.agg_recv.at[q], sibling)

    def aggregate(q):
        across(q).wait_recv()
        mine = (of("own", q)[...] + of("z_in", q)[...].astype(F32)).astype(BF16)
        s.agg[core, :, starts[q] : starts[q] + WIDTHS[q]] = mine
        agg_copy(q, core).start()
        return jnp.dot(mine, weight[starts[q] : starts[q] + WIDTHS[q], :], preferred_element_type=F32)

    slots = [[] for _ in range(2 * chunks + 4)]
    for q in range(chunks):
        slots[2 * q].append(lambda q=q: own_event(q))
        for step in range(4):
            slots[2 * q + 1 + step] += ring_events(q, step)
            slots[2 * q + 2 + step] += y_events(q, step)

    send_own(0)
    send_set()
    for q in range(1, chunks):
        send_own(q)
    work = []
    for slot, events in enumerate(slots):
        complete = slot // 2 - 3
        if slot == 6:
            work += [lambda: pair_arrivals(0), receive_table, lambda: receive_piece(0)] + multiplies(0, (0,))
            work += [lambda: receive_piece(1)] + multiplies(0, (1,))
        elif slot % 2 == 0 and 0 < complete < chunks - 1:
            work += [lambda q=complete: pair_arrivals(q)] + multiplies(complete, (0, 1))
        for event in events:
            event()
            if work:
                work.pop(0)()
    for item in work:
        item()
    receive_piece(2)
    for q in range(chunks - 1):
        for item in multiplies(q, (2,)):
            item()
        send_partial(q)
    pair_arrivals(chunks - 1)
    for item in multiplies(chunks - 1, (0, 1, 2)):
        item()
    send_partial(chunks - 1)
    for q in range(chunks - 1):
        sum_plane(q)
    for load in loads:
        load.wait()
    pre = aggregate(0)
    for q in range(1, chunks - 1):
        pre += aggregate(q)
    sum_plane(chunks - 1)
    pre += aggregate(chunks - 1)

    sigma = jax.nn.sigmoid(pre)
    s.slope[core] = (cotangent[...].astype(F32) * sigma * (1.0 + pre * (1.0 - sigma))).astype(BF16)
    slope_copy = remote(s.slope.at[core], s.slope.at[core], s.slope_sems.at[0], s.slope_sems.at[1], sibling)
    slope_copy.start()
    node_out[...] = (pre * sigma).astype(node_out.dtype)
    for q in range(chunks):
        agg_copy(q, 1 - core).wait_recv()
    slope_copy.wait_recv()

    columns = pl.ds(pl.multiple_of(core * 256, 256), 256)
    local = lax.dot_general(
        s.agg[:, :, columns].reshape(256, 256), s.slope[...].reshape(256, 512),
        (((0,), (0,)), ((), ())), preferred_element_type=F32,
    )
    s.grad[...] = local.reshape(16, 16, 512).astype(BF16)

    def grad_copy(step):
        there = spot_at(step)
        return remote(
            s.grad.at[there], s.grad_in.at[spot], s.grad_send.at[4 * step[0] + step[1]], s.grad_recv.at[spot],
            in_plane(step),
        )

    for step in FAR_FIRST:
        grad_copy(step).start()
    rows_sum = s.grad[spot].astype(F32)
    for step in reversed(FAR_FIRST):
        there = spot_at(step)
        ref = s.grad_in.at[there]
        remote(ref, ref, s.grad_send.at[0], s.grad_recv.at[there], sibling).wait_recv()
        rows_sum += s.grad_in[there].astype(F32)
    for j in range(8):
        s.piece[j] = rows_sum[8 * (j // 4) : 8 * (j // 4) + 8, 128 * (j % 4) : 128 * (j % 4) + 128]

    def piece_copy(distance):
        there = (z + distance) % 16
        return remote(
            s.piece.at[there % 8], s.piece_in.at[z], s.piece_send.at[distance], s.piece_recv.at[z],
            z_neighbour(x, y, zl, zh, core, distance),
        )

    for distance in (8, 7, 9, 6, 10, 5, 11, 4, 12, 3, 13, 2, 14, 1, 15):
        piece_copy(distance).start()
    s.piece_in[z] = s.piece[zl]
    for distance in range(1, 16):
        there = (z + distance) % 16
        ref = s.piece_in.at[there]
        remote(ref, ref, s.piece_send.at[0], s.piece_recv.at[there], sibling).wait_recv()
    result = s.piece_in[0]
    for j in range(1, 16):
        result += s.piece_in[j]
    s.total[...] = result
    s.total_in[zl] = result

    def total_copy(distance):
        return remote(
            s.total, s.total_in.at[zl], s.total_send.at[distance + 3], s.total_recv.at[zl],
            z_neighbour(x, y, zl, zh, core, distance),
        )

    near = (4, -3, 3, -2, 2, -1, 1)
    for distance in near:
        total_copy(distance).start()
    for distance in range(1, 8):
        there = (zl + distance) % 8
        remote(s.total, s.total_in.at[there], s.total_send.at[0], s.total_recv.at[there], sibling).wait_recv()
    upper = jnp.concatenate([s.total_in[j] for j in range(4)], axis=1)
    lower = jnp.concatenate([s.total_in[j] for j in range(4, 8)], axis=1)
    s.whole[core, spot] = jnp.concatenate([upper, lower], axis=0).astype(BF16)

    def whole_copy(step):
        ref = s.whole.at[core, spot]
        return remote(ref, ref, s.whole_send.at[4 * step[0] + step[1]], s.whole_recv.at[spot], in_plane(step))

    for step in FAR_FIRST:
        whole_copy(step).start()
    for step in reversed(FAR_FIRST):
        there = spot_at(step)
        ref = s.whole.at[core, there]
        remote(ref, ref, s.whole_send.at[0], s.whole_recv.at[there], sibling).wait_recv()
    final = remote(s.whole.at[core], s.whole.at[core], s.last_sems.at[0], s.last_sems.at[1], sibling)
    final.start()
    final.wait_recv()
    weight_grad[...] = s.whole[...].reshape(512, 512)

    for q in range(chunks):
        @pl.when(is_source)
        def _():
            own_remote(q, 0).wait_send()
            own_remote(q, 1).wait_send()

        for unit in (ALONE, BOTH):
            for upward in (True, False):
                for step in range(hops(q, unit, upward)):
                    hop(q, step, unit, upward).wait_send()
        for distance in (-4, -3, -2, -1, 1, 2, 3):
            y_copy(q, distance, ALONE).wait_send()
            for unit in (ALONE, BOTH, FROM_Y):
                pair_copy(q, distance, unit, core).wait_send()
        for distance in (1, 2, 3):
            to_owner(q, distance).wait_send()
        when_not(here, lambda: to_owner(q, 0).wait_send())
        across(q).wait_send()
        agg_copy(q, core).wait_send()

    @pl.when(jnp.logical_not(stays))
    def _():
        for i in range(PIECES + 1):
            set_remote(i).wait_send()

    slope_copy.wait_send()
    for step in FAR_FIRST:
        grad_copy(step).wait_send()
        whole_copy(step).wait_send()
    for distance in range(1, 16):
        piece_copy(distance).wait_send()
    for distance in near:
        total_copy(distance).wait_send()
    final.wait_send()


def shards(features, tiles, tile_rows, tile_cols, tile_count, weight, cotangent):
    vmem = pl.BlockSpec(memory_space=pltpu.VMEM)
    anywhere = pl.BlockSpec(memory_space=pl.ANY)
    node_out, weight_grad = pl.pallas_call(
        layer_kernel,
        out_shape=(
            jax.ShapeDtypeStruct(cotangent.shape, BF16),
            jax.ShapeDtypeStruct(weight.shape, BF16),
        ),
        in_specs=[anywhere, anywhere, vmem, vmem, vmem, anywhere, anywhere],
        out_specs=(vmem, vmem),
        scratch_shapes=list(scratch().values()),
        compiler_params=pltpu.CompilerParams(
            collective_id=0, has_side_effects=True, vmem_limit_bytes=60 * 2**20
        ),
        name="layer",
    )(
        features.reshape(8, 128, 512), tiles, tile_rows, tile_cols, tile_count, weight, cotangent,
    )
    return node_out, weight_grad.astype(F32)


def solution(mesh):
    in_specs = (
        P("dom", None),
        P(("dom", "rep"), None, None),
        P(("dom", "rep")),
        P(("dom", "rep")),
        P(("dom", "rep")),
        P(),
        P(("dom", "rep"), None),
    )
    out_specs = (P(("dom", "rep"), None), P())
    return jax.shard_map(shards, mesh=mesh, in_specs=in_specs, out_specs=out_specs, check_vma=False)
```

```python
import types

import jax
import jax.numpy as jnp
from jax import lax
from jax.experimental import pallas as pl
from jax.experimental.pallas import tpu as pltpu
from jax.sharding import PartitionSpec as P

MESH = pl.DeviceIdType.MESH
BF16 = jnp.bfloat16
F32 = jnp.float32
I32 = jnp.int32

WIDTHS = (256, 256)
ALONE, BOTH, FROM_Y = range(3)
SUMS = [(q, first) for q, width in enumerate(WIDTHS) for first in range(0, width, 128)]
SLOTS = 48
PIECES = 3
SLOT_STEP = 8
FAR_FIRST = sorted(
    [(dx, dy) for dx in range(4) for dy in range(4) if dx or dy],
    key=lambda d: -min(d[0], 4 - d[0]) - min(d[1], 4 - d[1]),
)


def at(x, y, zl, zh, core):
    return zl * 8 + x * 2 + core, zh * 4 + y


def hosted(x, y, zh, core):
    c = (2 * x + core + 16 - 4 * zh - y) % 8
    member = ((y + 1) // 2) % 2
    return c // 2, (1 - c % 2) * member + (c % 2) * (3 - member)


def set_of(host_x, host_y, zh, core):
    natural_core = host_y // 2
    member = (1 - natural_core) * host_y + natural_core * (3 - host_y)
    other = (core + natural_core) % 2
    y = (1 - other) * 2 * member + other * (3 - 2 * member)
    return ((2 * host_x + natural_core + 4 * zh + y - core) // 2) % 4, y


def place():
    dom, rep = lax.axis_index("dom"), lax.axis_index("rep")
    return (dom // 2) % 4, rep % 4, dom // 8, rep // 4, dom % 2


def z_neighbour(x, y, zl, zh, core, distance):
    z = (zh * 8 + zl + distance + 16) % 16
    return at(x, y, z % 8, z // 8, core)


def signal(device):
    pl.semaphore_signal(pltpu.get_barrier_semaphore(), inc=1, device_id=device, device_id_type=MESH)


def remote(src, dst, send, recv, device):
    return pltpu.make_async_remote_copy(
        src_ref=src, dst_ref=dst, send_sem=send, recv_sem=recv, device_id=device, device_id_type=MESH
    )


def when_not(condition, action):
    pl.when(jnp.logical_not(condition))(action)


def sort_slots(rows, cols, count, numbers):
    shape = (SLOTS, SLOTS)
    sub = lax.broadcasted_iota(I32, shape, 0).astype(F32)
    lane = lax.broadcasted_iota(I32, shape, 1).astype(F32)
    eye = (sub == lane).astype(F32)

    def column(row):
        return jnp.sum(eye * row, axis=1, keepdims=True)

    live = lane[:1] < count[...].reshape(1, 1).astype(F32)
    key = jnp.where(live, rows[...].reshape(1, SLOTS).astype(F32), 8.0)
    col = cols[...].reshape(1, SLOTS)
    block = ((col >> 6) * 8 + (col & 7)).astype(F32)
    unique = key * 64.0 + lane[:1]
    key_column = column(key)
    rank = jnp.sum((unique < column(unique)).astype(F32), axis=1, keepdims=True)
    chosen = (rank == lane).astype(F32)
    after = (rank + 1.0 == lane).astype(F32)
    sorted_key = jnp.sum(chosen * key_column, axis=0, keepdims=True)
    key_before = jnp.sum(after * key_column, axis=0, keepdims=True)
    numbers[0:1, 0:SLOTS] = jnp.sum(chosen * sub, axis=0, keepdims=True).astype(I32)
    numbers[1:2, 0:SLOTS] = jnp.sum(chosen * column(block), axis=0, keepdims=True).astype(I32)
    numbers[2:3, 0:SLOTS] = (sorted_key == key_before).astype(I32)
    ends = jnp.where(key_column == lane, rank + 1.0, 0.0)
    numbers[3:4, 0:SLOTS] = jnp.max(ends, axis=0, keepdims=True).astype(I32)


def scratch():
    vmem, sems = pltpu.VMEM, pltpu.SemaphoreType.DMA
    chunks = len(WIDTHS)
    names = {
        "numbers": vmem((8, 128), I32),
        "numbers_in": vmem((8, 128), I32),
        "own_table": pltpu.SMEM((8, 128), I32),
        "table": pltpu.SMEM((8, 128), I32),
        "tiles": vmem((SLOTS, 128, 128), BF16),
        "sorted_tiles": vmem((SLOTS, 128, 128), BF16),
        "tile_set": vmem((SLOTS, 128, 128), BF16),
        "weight": vmem((512, 512), BF16),
        "cotangent": vmem((128, 512), BF16),
        "load_sems": sems((2,)),
        "line_sems": pltpu.SemaphoreType.REGULAR((3,)),
        "agg": vmem((2, 128, 512), BF16),
        "slope": vmem((2, 128, 512), BF16),
        "grad": vmem((16, 16, 512), BF16),
        "grad_in": vmem((16, 16, 512), BF16),
        "piece": vmem((8, 8, 128), F32),
        "piece_in": vmem((16, 8, 128), F32),
        "total": vmem((8, 128), F32),
        "total_in": vmem((8, 8, 128), F32),
        "whole": vmem((2, 16, 16, 512), BF16),
        "set_send": sems((PIECES + 1,)),
        "set_recv": sems((PIECES + 1,)),
        "local_sems": sems((3,)),
        "own_send": sems((chunks, 2)),
        "own_recv": sems((chunks, 2)),
        "ring_send": sems((chunks, 2, 4, 2)),
        "ring_recv": sems((chunks, 2, 4, 2)),
        "y_send": sems((chunks, 8)),
        "y_recv": sems((chunks, 8)),
        "y_other_send": sems((chunks,)),
        "pair_send": sems((chunks, 8, 3)),
        "pair_recv": sems((chunks, 8, 3)),
        "plane_send": sems((len(SUMS), 4)),
        "plane_recv": sems((len(SUMS), 4)),
        "z_send": sems((len(SUMS),)),
        "z_recv": sems((len(SUMS),)),
        "agg_send": sems((len(SUMS),)),
        "agg_recv": sems((len(SUMS),)),
        "slope_sems": sems((2,)),
        "grad_send": sems((16,)),
        "grad_recv": sems((16,)),
        "piece_send": sems((16,)),
        "piece_recv": sems((16,)),
        "total_send": sems((8,)),
        "total_recv": sems((8,)),
        "whole_send": sems((16,)),
        "whole_recv": sems((16,)),
        "last_send": sems((16,)),
        "last_recv": sems((16,)),
    }
    for q, width in enumerate(WIDTHS):
        names["blocks%d" % q] = vmem((64, 128, width), BF16)
        names["products%d" % q] = vmem((SLOTS + 1, 128, width), F32)
    for part in range(len(SUMS)):
        names["partial%d" % part] = vmem((2, 4, 128, 128), BF16)
        names["plane_in%d" % part] = vmem((4, 2, 128, 128), BF16)
        names["z_out%d" % part] = vmem((128, 128), BF16)
        names["z_in%d" % part] = vmem((128, 128), BF16)
        names["own%d" % part] = vmem((128, 128), F32)
    return names


def layer_kernel(features, tiles_in, rows, cols, count, weight_in, cotangent_in, node_out, weight_grad, *refs):
    s = types.SimpleNamespace(**dict(zip(scratch(), refs)))
    chunks = len(WIDTHS)
    starts = [sum(WIDTHS[:q]) for q in range(chunks)]

    def of(name, q):
        return getattr(s, name + str(q))

    x, y, zl, zh, core = place()
    z = zh * 8 + zl
    spot = x * 4 + y
    sibling = at(x, y, zl, zh, 1 - core)
    up = z_neighbour(x, y, zl, zh, core, 1)
    down = z_neighbour(x, y, zl, zh, core, -1)
    natural_core = y // 2
    is_source = core == natural_core
    member = y % 2
    y_pair = at(x, y + 1 - 2 * member, zl, zh, core)
    y_pair_other = at(x, y + 1 - 2 * member, zl, zh, 1 - core)

    def in_plane(step):
        return at((x + step[0]) % 4, (y + step[1]) % 4, zl, zh, core)

    def spot_at(step):
        return (x + step[0]) % 4 * 4 + (y + step[1]) % 4

    weight, cotangent = s.weight, s.cotangent
    loads = [
        pltpu.make_async_copy(weight_in, weight, s.load_sems.at[0]),
        pltpu.make_async_copy(cotangent_in, cotangent, s.load_sems.at[1]),
    ]
    load_tiles = pltpu.make_async_copy(tiles_in, s.tiles, s.local_sems.at[0])
    load_tiles.start()

    signal(up)
    signal(down)
    signal(sibling)
    signal(y_pair_other)
    for step in FAR_FIRST:
        signal(in_plane(step))
    def entry(table, row, place, top):
        return jnp.minimum(jnp.maximum(table[row, place], 0), top)

    def place_tile(j, carry):
        s.sorted_tiles[j] = s.tiles[entry(s.own_table, 0, j, SLOTS - 1)]
        return carry

    sort_slots(rows, cols, count, s.numbers)
    to_own_table = pltpu.make_async_copy(s.numbers, s.own_table, s.local_sems.at[1])
    to_own_table.start()
    load_tiles.wait()
    to_own_table.wait()
    lax.fori_loop(0, SLOTS, place_tile, 0, unroll=2)

    pl.semaphore_wait(pltpu.get_barrier_semaphore(), 19)

    def greet(i):
        for distance in (2**i, -(2**i)):
            pl.semaphore_signal(
                s.line_sems.at[i], inc=1, device_id=z_neighbour(x, y, zl, zh, core, distance), device_id_type=MESH
            )

    def greeted(i):
        pl.semaphore_wait(s.line_sems.at[i], 2)

    greet(0)

    def block_rows(distance, of_core):
        return (zl + distance + 8) % 8 * 8 + of_core * 4

    def block_part(q, distance, unit, of_core):
        row = block_rows(distance, of_core)
        row = row + (member if unit == ALONE else 2 if unit == BOTH else 1 - member)
        return of("blocks", q).at[pl.ds(row, 2 if unit == BOTH else 1)]

    def own_part(q, of_core):
        columns = pl.ds(starts[q], WIDTHS[q])
        return features.at[pl.ds(of_core * 4, 4), :, columns], of("blocks", q).at[pl.ds(block_rows(0, of_core), 4)]

    def own_local(q, of_core):
        return pltpu.make_async_copy(*own_part(q, of_core), s.own_recv.at[q, of_core])

    def own_remote(q, of_core):
        return remote(*own_part(q, of_core), s.own_send.at[q, of_core], s.own_recv.at[q, of_core], sibling)

    def send_own(q):
        @pl.when(is_source)
        def _():
            own_remote(q, 1 - core).start()
            own_local(q, core).start()
            own_remote(q, core).start()
            own_local(q, 1 - core).start()

    def hop(q, step, unit, upward):
        ref = block_part(q, -step if upward else step, unit, core)
        way = 0 if upward else 1
        return remote(
            ref, ref, s.ring_send.at[q, way, step, unit], s.ring_recv.at[q, way, step, unit], up if upward else down
        )

    def arrival(q, step, unit, upward):
        ref = block_part(q, -step - 1 if upward else step + 1, unit, core)
        way = 0 if upward else 1
        return remote(ref, ref, s.ring_send.at[q, way, step, unit], s.ring_recv.at[q, way, step, unit], sibling)

    def y_copy(q, distance, unit):
        ref = block_part(q, distance, unit, core)
        return remote(ref, ref, s.y_send.at[q, distance + 4], s.y_recv.at[q, distance + 4], y_pair)

    def y_other_copy(q):
        ref = block_part(q, -4, ALONE, core)
        return remote(ref, ref, s.y_other_send.at[q], s.pair_recv.at[q, 0, FROM_Y], y_pair_other)

    def pair_copy(q, distance, unit, of_core):
        ref = block_part(q, distance, unit, of_core)
        return remote(ref, ref, s.pair_send.at[q, distance + 4, unit], s.pair_recv.at[q, distance + 4, unit], sibling)

    def hops(q, unit, upward):
        return 4 if (unit == (ALONE if q % 2 == 0 else BOTH)) == upward else 3

    def own_event(q):
        own_local(q, core).wait()
        for unit in (ALONE, BOTH):
            hop(q, 0, unit, True).start()
            hop(q, 0, unit, False).start()

    def ring_event(q, step, unit, upward):
        arrival(q, step, unit, upward).wait_recv()
        if step + 1 < hops(q, unit, upward):
            hop(q, step + 1, unit, upward).start()
        distance = -step - 1 if upward or step == 3 else step + 1
        if unit == ALONE:
            y_copy(q, distance, ALONE).start()
            if distance == -4:
                y_other_copy(q).start()
        pair_copy(q, distance, unit, core).start()

    def y_event(q, distance):
        y_copy(q, distance, FROM_Y).wait_recv()
        if distance != -4:
            pair_copy(q, distance, FROM_Y, core).start()

    def ring_events(q, step):
        return [
            lambda unit=unit, upward=upward: ring_event(q, step, unit, upward)
            for unit in (ALONE, BOTH)
            for upward in (True, False)
            if step < hops(q, unit, upward)
        ]

    def y_events(q, step):
        distances = (-4,) if step == 3 else (-step - 1, step + 1)
        return [lambda distance=distance: y_event(q, distance) for distance in distances]

    def pair_arrivals(q):
        own_local(q, 1 - core).wait()
        for distance in (-1, 1, -2, 2, -3, 3, -4):
            for unit in (ALONE, BOTH, FROM_Y):
                pair_copy(q, distance, unit, 1 - core).wait_recv()

    host_x, host_y = hosted(x, y, zh, core)
    stays = (host_x + 4 - x) % 4 + (host_y + 4 - y) % 4 == 0
    host = at(host_x, host_y, zl, zh, core)
    per_piece = SLOTS // PIECES
    set_parts = [(s.numbers, s.numbers_in)] + [
        (s.sorted_tiles.at[pl.ds(i * per_piece, per_piece)], s.tile_set.at[pl.ds(i * per_piece, per_piece)])
        for i in range(PIECES)
    ]

    def set_remote(i):
        return remote(*set_parts[i], s.set_send.at[i], s.set_recv.at[i], host)

    def set_local(i):
        return pltpu.make_async_copy(*set_parts[i], s.set_recv.at[i])

    def send_set():
        @pl.when(stays)
        def _():
            for i in range(PIECES + 1):
                set_local(i).start()

        @pl.when(jnp.logical_not(stays))
        def _():
            for i in range(PIECES + 1):
                set_remote(i).start()

    def receive_table():
        set_local(0).wait()
        to_table = pltpu.make_async_copy(s.numbers_in, s.table, s.local_sems.at[2])
        to_table.start()
        to_table.wait()

    def receive_piece(i):
        set_local(i + 1).wait()

    def multiply(q, first):
        def four(i, carry):
            base = first + 4 * i
            total = of("products", q)[base]
            for j in range(4):
                block = of("blocks", q)[entry(s.table, 1, base + j, 63)]
                product = jnp.dot(s.tile_set[base + j], block, preferred_element_type=F32)
                total = product + s.table[2, base + j].astype(F32) * total
                of("products", q)[base + j + 1] = total
            return carry

        lax.fori_loop(0, SLOT_STEP // 4, four, 0)

    def multiplies(q, pieces):
        slots = range(pieces[0] * per_piece, (pieces[-1] + 1) * per_piece, SLOT_STEP)
        return [lambda first=first: multiply(q, first) for first in slots]

    set_x, set_y = set_of(x, y, zh, core)
    here = (set_x + 4 - x) % 4 == 0

    def to_owner(part, distance):
        there = (y + distance) % 4
        return remote(
            of("partial", part).at[:, there], of("plane_in", part).at[set_y], s.plane_send.at[part, distance],
            s.plane_recv.at[part, set_y], at(set_x, there, zl, zh, core),
        )

    def send_partial(part):
        q, first = SUMS[part]
        for t in range(8):
            sums = of("products", q)[entry(s.table, 3, t, SLOTS), :, first : first + 128]
            of("partial", part)[t // 4, t % 4] = sums.astype(BF16)
        for distance in (2, 1, 3):
            to_owner(part, distance).start()

        @pl.when(here)
        def _():
            pltpu.make_async_copy(
                of("partial", part).at[:, y], of("plane_in", part).at[set_y], s.plane_recv.at[part, set_y]
            ).start()

        when_not(here, lambda: to_owner(part, 0).start())

    def across(part):
        return remote(
            of("z_out", part), of("z_in", part), s.z_send.at[part], s.z_recv.at[part], z_neighbour(x, y, zl, zh, core, 8)
        )

    def sum_plane(part):
        for member in range(4):
            ref = of("plane_in", part).at[member]
            remote(ref, ref, s.plane_send.at[part, 0], s.plane_recv.at[part, member], sibling).wait_recv()

        def summed(half):
            result = of("plane_in", part)[0, half].astype(F32)
            for member in range(1, 4):
                result += of("plane_in", part)[member, half].astype(F32)
            return result

        of("z_out", part)[...] = summed(1 - zh).astype(BF16)
        across(part).start()
        of("own", part)[...] = summed(zh)

    def agg_copy(part, of_core):
        ref = s.agg.at[of_core, :, pl.ds(128 * part, 128)]
        return remote(ref, ref, s.agg_send.at[part], s.agg_recv.at[part], sibling)

    def aggregate(part):
        across(part).wait_recv()
        mine = (of("own", part)[...] + of("z_in", part)[...].astype(F32)).astype(BF16)
        s.agg[core, :, 128 * part : 128 * part + 128] = mine
        agg_copy(part, core).start()
        return jnp.dot(mine, weight[128 * part : 128 * part + 128, :], preferred_element_type=F32)

    def send_sums(q):
        for part, (of_columns, _) in enumerate(SUMS):
            if of_columns == q:
                send_partial(part)

    def drain_features(q):
        @pl.when(is_source)
        def _():
            own_remote(q, 0).wait_send()
            own_remote(q, 1).wait_send()

        for unit in (ALONE, BOTH):
            for upward in (True, False):
                for step in range(hops(q, unit, upward)):
                    hop(q, step, unit, upward).wait_send()
        for distance in (-4, -3, -2, -1, 1, 2, 3):
            y_copy(q, distance, ALONE).wait_send()
            for unit in (ALONE, BOTH, FROM_Y):
                if unit != FROM_Y or distance != -4:
                    pair_copy(q, distance, unit, core).wait_send()
        y_other_copy(q).wait_send()

    def drain_set():
        @pl.when(jnp.logical_not(stays))
        def _():
            for i in range(PIECES + 1):
                set_remote(i).wait_send()

    def drain_sums(part):
        for distance in (1, 2, 3):
            to_owner(part, distance).wait_send()
        when_not(here, lambda: to_owner(part, 0).wait_send())
        across(part).wait_send()
        agg_copy(part, core).wait_send()

    slots = [[] for _ in range(2 * chunks + 4)]
    for q in range(chunks):
        slots[2 * q].append(lambda q=q: own_event(q))
        for step in range(4):
            slots[2 * q + 1 + step] += ring_events(q, step)
            slots[2 * q + 2 + step] += y_events(q, step)

    send_own(0)
    send_set()
    for event in slots.pop(0):
        event()
    for q in range(1, chunks):
        send_own(q)
    for load in loads:
        load.start()
    for q in range(chunks):
        of("products", q)[0] = jnp.zeros((128, WIDTHS[q]), F32)
    work = []
    for slot, events in enumerate(slots, 1):
        complete = slot // 2 - 3
        if slot in (2, 4, 6):
            greeted(slot // 2 - 1)
            if slot < 6:
                greet(slot // 2)
        if slot == 6:
            work += [lambda: pair_arrivals(0), receive_table, lambda: receive_piece(0)] + multiplies(0, (0,))
            work += [lambda: receive_piece(1)] + multiplies(0, (1,))
        elif slot % 2 == 0 and 0 < complete < chunks - 1:
            work += [lambda q=complete: pair_arrivals(q)] + multiplies(complete, (0, 1))
        for event in events:
            event()
            if work:
                work.pop(0)()
    for item in work:
        item()
    receive_piece(2)
    for q in range(chunks - 1):
        for item in multiplies(q, (2,)):
            item()
        send_sums(q)
    pair_arrivals(chunks - 1)
    for item in multiplies(chunks - 1, (0, 1, 2)):
        item()
    send_sums(chunks - 1)
    for q in range(chunks):
        drain_features(q)
    drain_set()
    for load in loads:
        load.wait()
    for part in range(len(SUMS)):
        sum_plane(part)
    pre = aggregate(0)
    for part in range(1, len(SUMS)):
        pre += aggregate(part)

    sigma = jax.nn.sigmoid(pre)
    s.slope[core] = (cotangent[...].astype(F32) * sigma * (1.0 + pre * (1.0 - sigma))).astype(BF16)
    slope_copy = remote(s.slope.at[core], s.slope.at[core], s.slope_sems.at[0], s.slope_sems.at[1], sibling)
    slope_copy.start()
    node_out[...] = (pre * sigma).astype(node_out.dtype)
    for part in range(len(SUMS)):
        agg_copy(part, 1 - core).wait_recv()
    slope_copy.wait_recv()

    columns = pl.ds(pl.multiple_of(core * 256, 256), 256)
    local = lax.dot_general(
        s.agg[:, :, columns].reshape(256, 256), s.slope[...].reshape(256, 512),
        (((0,), (0,)), ((), ())), preferred_element_type=F32,
    )
    s.grad[...] = local.reshape(16, 16, 512).astype(BF16)

    def grad_copy(step):
        there = spot_at(step)
        return remote(
            s.grad.at[there], s.grad_in.at[spot], s.grad_send.at[4 * step[0] + step[1]], s.grad_recv.at[spot],
            in_plane(step),
        )

    for step in FAR_FIRST:
        grad_copy(step).start()
    slope_copy.wait_send()
    for part in range(len(SUMS)):
        drain_sums(part)
    rows_sum = s.grad[spot].astype(F32)
    for step in reversed(FAR_FIRST):
        there = spot_at(step)
        ref = s.grad_in.at[there]
        remote(ref, ref, s.grad_send.at[0], s.grad_recv.at[there], sibling).wait_recv()
        rows_sum += s.grad_in[there].astype(F32)
    for j in range(8):
        s.piece[j] = rows_sum[8 * (j // 4) : 8 * (j // 4) + 8, 128 * (j % 4) : 128 * (j % 4) + 128]

    def piece_copy(distance):
        there = (z + distance) % 16
        return remote(
            s.piece.at[there % 8], s.piece_in.at[z], s.piece_send.at[distance], s.piece_recv.at[z],
            z_neighbour(x, y, zl, zh, core, distance),
        )

    for distance in (8, 7, 9, 6, 10, 5, 11, 4, 12, 3, 13, 2, 14, 1, 15):
        piece_copy(distance).start()
    s.piece_in[z] = s.piece[zl]
    for step in FAR_FIRST:
        grad_copy(step).wait_send()
    for distance in range(1, 16):
        there = (z + distance) % 16
        ref = s.piece_in.at[there]
        remote(ref, ref, s.piece_send.at[0], s.piece_recv.at[there], sibling).wait_recv()
    result = s.piece_in[0]
    for j in range(1, 16):
        result += s.piece_in[j]
    s.total[...] = result
    s.total_in[zl] = result

    def total_copy(distance):
        return remote(
            s.total, s.total_in.at[zl], s.total_send.at[distance + 3], s.total_recv.at[zl],
            z_neighbour(x, y, zl, zh, core, distance),
        )

    near = (4, -3, 3, -2, 2, -1, 1)
    for distance in near:
        total_copy(distance).start()
    for distance in range(1, 16):
        piece_copy(distance).wait_send()
    for distance in range(1, 8):
        there = (zl + distance) % 8
        remote(s.total, s.total_in.at[there], s.total_send.at[0], s.total_recv.at[there], sibling).wait_recv()
    upper = jnp.concatenate([s.total_in[j] for j in range(4)], axis=1)
    lower = jnp.concatenate([s.total_in[j] for j in range(4, 8)], axis=1)
    s.whole[core, spot] = jnp.concatenate([upper, lower], axis=0).astype(BF16)

    def whole_copy(step):
        ref = s.whole.at[core, spot]
        return remote(ref, ref, s.whole_send.at[4 * step[0] + step[1]], s.whole_recv.at[spot], in_plane(step))

    def last_copy(n, of_core):
        ref = s.whole.at[of_core, n]
        return remote(ref, ref, s.last_send.at[n], s.last_recv.at[n], sibling)

    for step in FAR_FIRST:
        whole_copy(step).start()
    last_copy(spot, core).start()
    for distance in near:
        total_copy(distance).wait_send()
    for step in reversed(FAR_FIRST):
        there = spot_at(step)
        ref = s.whole.at[core, there]
        remote(ref, ref, s.whole_send.at[0], s.whole_recv.at[there], sibling).wait_recv()
        last_copy(there, core).start()
    for n in range(16):
        last_copy(n, 1 - core).wait_recv()
    weight_grad[...] = s.whole[...].reshape(512, 512)

    for step in FAR_FIRST:
        whole_copy(step).wait_send()
    for n in range(16):
        last_copy(n, core).wait_send()


def shards(features, tiles, tile_rows, tile_cols, tile_count, weight, cotangent):
    vmem = pl.BlockSpec(memory_space=pltpu.VMEM)
    anywhere = pl.BlockSpec(memory_space=pl.ANY)
    node_out, weight_grad = pl.pallas_call(
        layer_kernel,
        out_shape=(
            jax.ShapeDtypeStruct(cotangent.shape, BF16),
            jax.ShapeDtypeStruct(weight.shape, BF16),
        ),
        in_specs=[anywhere, anywhere, vmem, vmem, vmem, anywhere, anywhere],
        out_specs=(vmem, vmem),
        scratch_shapes=list(scratch().values()),
        compiler_params=pltpu.CompilerParams(
            collective_id=0, has_side_effects=True, vmem_limit_bytes=60 * 2**20
        ),
        name="layer",
    )(
        features.reshape(8, 128, 512), tiles, tile_rows, tile_cols, tile_count, weight, cotangent,
    )
    return node_out, weight_grad.astype(F32)


def solution(mesh):
    in_specs = (
        P("dom", None),
        P(("dom", "rep"), None, None),
        P(("dom", "rep")),
        P(("dom", "rep")),
        P(("dom", "rep")),
        P(),
        P(("dom", "rep"), None),
    )
    out_specs = (P(("dom", "rep"), None), P())
    return jax.shard_map(shards, mesh=mesh, in_specs=in_specs, out_specs=out_specs, check_vma=False)
```

```python
import types

import jax
import jax.numpy as jnp
from jax import lax
from jax.experimental import pallas as pl
from jax.experimental.pallas import tpu as pltpu
from jax.sharding import PartitionSpec as P

MESH = pl.DeviceIdType.MESH
BF16 = jnp.bfloat16
F32 = jnp.float32
I32 = jnp.int32

WIDTHS = (256, 256)
ALONE, BOTH, FROM_Y = range(3)
SUMS = [(q, first) for q, width in enumerate(WIDTHS) for first in range(0, width, 128)]
SLOTS = 48
PIECES = 3
SLOT_STEP = 8
FAR_FIRST = sorted(
    [(dx, dy) for dx in range(4) for dy in range(4) if dx or dy],
    key=lambda d: -min(d[0], 4 - d[0]) - min(d[1], 4 - d[1]),
)


def at(x, y, zl, zh, core):
    return zl * 8 + x * 2 + core, zh * 4 + y


def hosted(x, y, zh, core):
    c = (2 * x + core + 16 - 4 * zh - y) % 8
    member = ((y + 1) // 2) % 2
    return c // 2, (1 - c % 2) * member + (c % 2) * (3 - member)


def set_of(host_x, host_y, zh, core):
    natural_core = host_y // 2
    member = (1 - natural_core) * host_y + natural_core * (3 - host_y)
    other = (core + natural_core) % 2
    y = (1 - other) * 2 * member + other * (3 - 2 * member)
    return ((2 * host_x + natural_core + 4 * zh + y - core) // 2) % 4, y


def place():
    dom, rep = lax.axis_index("dom"), lax.axis_index("rep")
    return (dom // 2) % 4, rep % 4, dom // 8, rep // 4, dom % 2


def z_neighbour(x, y, zl, zh, core, distance):
    z = (zh * 8 + zl + distance + 16) % 16
    return at(x, y, z % 8, z // 8, core)


def signal(device):
    pl.semaphore_signal(pltpu.get_barrier_semaphore(), inc=1, device_id=device, device_id_type=MESH)


def remote(src, dst, send, recv, device):
    return pltpu.make_async_remote_copy(
        src_ref=src, dst_ref=dst, send_sem=send, recv_sem=recv, device_id=device, device_id_type=MESH
    )


def when_not(condition, action):
    pl.when(jnp.logical_not(condition))(action)


def sort_slots(rows, cols, count, numbers):
    shape = (SLOTS, SLOTS)
    sub = lax.broadcasted_iota(I32, shape, 0).astype(F32)
    lane = lax.broadcasted_iota(I32, shape, 1).astype(F32)
    eye = (sub == lane).astype(F32)

    def column(row):
        return jnp.sum(eye * row, axis=1, keepdims=True)

    live = lane[:1] < count[...].reshape(1, 1).astype(F32)
    key = jnp.where(live, rows[...].reshape(1, SLOTS).astype(F32), 8.0)
    col = cols[...].reshape(1, SLOTS)
    block = ((col >> 6) * 8 + (col & 7)).astype(F32)
    unique = key * 64.0 + lane[:1]
    key_column = column(key)
    rank = jnp.sum((unique < column(unique)).astype(F32), axis=1, keepdims=True)
    chosen = (rank == lane).astype(F32)
    after = (rank + 1.0 == lane).astype(F32)
    sorted_key = jnp.sum(chosen * key_column, axis=0, keepdims=True)
    key_before = jnp.sum(after * key_column, axis=0, keepdims=True)
    numbers[0:1, 0:SLOTS] = jnp.sum(chosen * sub, axis=0, keepdims=True).astype(I32)
    numbers[1:2, 0:SLOTS] = jnp.sum(chosen * column(block), axis=0, keepdims=True).astype(I32)
    numbers[2:3, 0:SLOTS] = (sorted_key == key_before).astype(I32)
    ends = jnp.where(key_column == lane, rank + 1.0, 0.0)
    numbers[3:4, 0:SLOTS] = jnp.max(ends, axis=0, keepdims=True).astype(I32)


def scratch():
    vmem, sems = pltpu.VMEM, pltpu.SemaphoreType.DMA
    chunks = len(WIDTHS)
    names = {
        "numbers": vmem((8, 128), I32),
        "numbers_in": vmem((8, 128), I32),
        "own_table": pltpu.SMEM((8, 128), I32),
        "table": pltpu.SMEM((8, 128), I32),
        "tiles": vmem((SLOTS, 128, 128), BF16),
        "sorted_tiles": vmem((SLOTS, 128, 128), BF16),
        "tile_set": vmem((SLOTS, 128, 128), BF16),
        "weight": vmem((512, 512), BF16),
        "cotangent": vmem((128, 512), BF16),
        "load_sems": sems((2,)),
        "line_sems": pltpu.SemaphoreType.REGULAR((3,)),
        "agg": vmem((2, 128, 512), BF16),
        "slope": vmem((2, 128, 512), BF16),
        "grad": vmem((16, 16, 512), BF16),
        "grad_in": vmem((16, 16, 512), BF16),
        "piece": vmem((8, 8, 128), F32),
        "piece_in": vmem((16, 8, 128), F32),
        "total": vmem((8, 128), F32),
        "total_in": vmem((8, 8, 128), F32),
        "whole": vmem((2, 16, 16, 512), BF16),
        "set_send": sems((PIECES + 1,)),
        "set_recv": sems((PIECES + 1,)),
        "local_sems": sems((3,)),
        "own_send": sems((chunks, 2)),
        "own_recv": sems((chunks, 2)),
        "ring_send": sems((chunks, 2, 4, 2)),
        "ring_recv": sems((chunks, 2, 4, 2)),
        "y_send": sems((chunks, 8)),
        "y_recv": sems((chunks, 8)),
        "y_other_send": sems((chunks,)),
        "pair_send": sems((chunks, 8, 3)),
        "pair_recv": sems((chunks, 8, 3)),
        "plane_send": sems((len(SUMS), 4)),
        "plane_recv": sems((len(SUMS), 4)),
        "z_send": sems((len(SUMS),)),
        "z_recv": sems((len(SUMS),)),
        "agg_send": sems((len(SUMS),)),
        "agg_recv": sems((len(SUMS),)),
        "slope_sems": sems((2,)),
        "grad_send": sems((16,)),
        "grad_recv": sems((16,)),
        "piece_send": sems((16,)),
        "piece_recv": sems((16,)),
        "total_send": sems((8,)),
        "total_recv": sems((8,)),
        "whole_send": sems((16,)),
        "whole_recv": sems((16,)),
        "last_send": sems((16,)),
        "last_recv": sems((16,)),
    }
    for q, width in enumerate(WIDTHS):
        names["blocks%d" % q] = vmem((64, 128, width), BF16)
        names["products%d" % q] = vmem((SLOTS + 1, 128, width), F32)
    for part in range(len(SUMS)):
        names["partial%d" % part] = vmem((2, 4, 128, 128), BF16)
        names["plane_in%d" % part] = vmem((4, 2, 128, 128), BF16)
        names["z_out%d" % part] = vmem((128, 128), BF16)
        names["z_in%d" % part] = vmem((128, 128), BF16)
        names["own%d" % part] = vmem((128, 128), F32)
    return names


def layer_kernel(features, tiles_in, rows, cols, count, weight_in, cotangent_in, node_out, weight_grad, *refs):
    s = types.SimpleNamespace(**dict(zip(scratch(), refs)))
    chunks = len(WIDTHS)
    starts = [sum(WIDTHS[:q]) for q in range(chunks)]

    def of(name, q):
        return getattr(s, name + str(q))

    x, y, zl, zh, core = place()
    z = zh * 8 + zl
    spot = x * 4 + y
    sibling = at(x, y, zl, zh, 1 - core)
    up = z_neighbour(x, y, zl, zh, core, 1)
    down = z_neighbour(x, y, zl, zh, core, -1)
    natural_core = y // 2
    is_source = core == natural_core
    member = y % 2
    y_pair = at(x, y + 1 - 2 * member, zl, zh, core)
    y_pair_other = at(x, y + 1 - 2 * member, zl, zh, 1 - core)

    def in_plane(step):
        return at((x + step[0]) % 4, (y + step[1]) % 4, zl, zh, core)

    def spot_at(step):
        return (x + step[0]) % 4 * 4 + (y + step[1]) % 4

    weight, cotangent = s.weight, s.cotangent
    loads = [
        pltpu.make_async_copy(weight_in, weight, s.load_sems.at[0]),
        pltpu.make_async_copy(cotangent_in, cotangent, s.load_sems.at[1]),
    ]
    load_tiles = pltpu.make_async_copy(tiles_in, s.tiles, s.local_sems.at[0])
    load_tiles.start()

    signal(up)
    signal(down)
    signal(sibling)
    signal(y_pair_other)
    for step in FAR_FIRST:
        signal(in_plane(step))
    def entry(table, row, place, top):
        return jnp.minimum(jnp.maximum(table[row, place], 0), top)

    def place_tile(j, carry):
        s.sorted_tiles[j] = s.tiles[entry(s.own_table, 0, j, SLOTS - 1)]
        return carry

    sort_slots(rows, cols, count, s.numbers)
    to_own_table = pltpu.make_async_copy(s.numbers, s.own_table, s.local_sems.at[1])
    to_own_table.start()
    load_tiles.wait()
    to_own_table.wait()
    lax.fori_loop(0, SLOTS, place_tile, 0, unroll=2)

    pl.semaphore_wait(pltpu.get_barrier_semaphore(), 19)

    def greet(i):
        for distance in (2**i, -(2**i)):
            pl.semaphore_signal(
                s.line_sems.at[i], inc=1, device_id=z_neighbour(x, y, zl, zh, core, distance), device_id_type=MESH
            )

    def greeted(i):
        pl.semaphore_wait(s.line_sems.at[i], 2)

    greet(0)

    def block_rows(distance, of_core):
        return (zl + distance + 8) % 8 * 8 + of_core * 4

    def block_part(q, distance, unit, of_core):
        row = block_rows(distance, of_core)
        row = row + (member if unit == ALONE else 2 if unit == BOTH else 1 - member)
        return of("blocks", q).at[pl.ds(row, 2 if unit == BOTH else 1)]

    def own_part(q, of_core):
        columns = pl.ds(starts[q], WIDTHS[q])
        return features.at[pl.ds(of_core * 4, 4), :, columns], of("blocks", q).at[pl.ds(block_rows(0, of_core), 4)]

    def own_local(q, of_core):
        return pltpu.make_async_copy(*own_part(q, of_core), s.own_recv.at[q, of_core])

    def own_remote(q, of_core):
        return remote(*own_part(q, of_core), s.own_send.at[q, of_core], s.own_recv.at[q, of_core], sibling)

    def send_own(q):
        @pl.when(is_source)
        def _():
            own_remote(q, 1 - core).start()
            own_local(q, core).start()
            own_remote(q, core).start()
            own_local(q, 1 - core).start()

    def hop(q, step, unit, upward):
        ref = block_part(q, -step if upward else step, unit, core)
        way = 0 if upward else 1
        return remote(
            ref, ref, s.ring_send.at[q, way, step, unit], s.ring_recv.at[q, way, step, unit], up if upward else down
        )

    def arrival(q, step, unit, upward):
        ref = block_part(q, -step - 1 if upward else step + 1, unit, core)
        way = 0 if upward else 1
        return remote(ref, ref, s.ring_send.at[q, way, step, unit], s.ring_recv.at[q, way, step, unit], sibling)

    def y_copy(q, distance, unit):
        ref = block_part(q, distance, unit, core)
        return remote(ref, ref, s.y_send.at[q, distance + 4], s.y_recv.at[q, distance + 4], y_pair)

    def y_other_copy(q):
        ref = block_part(q, -4, ALONE, core)
        return remote(ref, ref, s.y_other_send.at[q], s.pair_recv.at[q, 0, FROM_Y], y_pair_other)

    def pair_copy(q, distance, unit, of_core):
        ref = block_part(q, distance, unit, of_core)
        return remote(ref, ref, s.pair_send.at[q, distance + 4, unit], s.pair_recv.at[q, distance + 4, unit], sibling)

    def hops(q, unit, upward):
        return 4 if (unit == (ALONE if q % 2 == 0 else BOTH)) == upward else 3

    def own_event(q):
        own_local(q, core).wait()
        for unit in (ALONE, BOTH):
            hop(q, 0, unit, True).start()
            hop(q, 0, unit, False).start()

    def ring_event(q, step, unit, upward):
        arrival(q, step, unit, upward).wait_recv()
        if step + 1 < hops(q, unit, upward):
            hop(q, step + 1, unit, upward).start()
        distance = -step - 1 if upward or step == 3 else step + 1
        if unit == ALONE:
            y_copy(q, distance, ALONE).start()
            if distance == -4:
                y_other_copy(q).start()
        pair_copy(q, distance, unit, core).start()

    def y_event(q, distance):
        y_copy(q, distance, FROM_Y).wait_recv()
        if distance != -4:
            pair_copy(q, distance, FROM_Y, core).start()

    def ring_events(q, step):
        return [
            lambda unit=unit, upward=upward: ring_event(q, step, unit, upward)
            for unit in (ALONE, BOTH)
            for upward in (True, False)
            if step < hops(q, unit, upward)
        ]

    def y_events(q, step):
        distances = (-4,) if step == 3 else (-step - 1, step + 1)
        return [lambda distance=distance: y_event(q, distance) for distance in distances]

    def pair_arrivals(q):
        own_local(q, 1 - core).wait()
        for distance in (-1, 1, -2, 2, -3, 3, -4):
            for unit in (ALONE, BOTH, FROM_Y):
                pair_copy(q, distance, unit, 1 - core).wait_recv()

    host_x, host_y = hosted(x, y, zh, core)
    stays = (host_x + 4 - x) % 4 + (host_y + 4 - y) % 4 == 0
    host = at(host_x, host_y, zl, zh, core)
    per_piece = SLOTS // PIECES
    set_parts = [(s.numbers, s.numbers_in)] + [
        (s.sorted_tiles.at[pl.ds(i * per_piece, per_piece)], s.tile_set.at[pl.ds(i * per_piece, per_piece)])
        for i in range(PIECES)
    ]

    def set_remote(i):
        return remote(*set_parts[i], s.set_send.at[i], s.set_recv.at[i], host)

    def set_local(i):
        return pltpu.make_async_copy(*set_parts[i], s.set_recv.at[i])

    def send_set():
        @pl.when(stays)
        def _():
            for i in range(PIECES + 1):
                set_local(i).start()

        @pl.when(jnp.logical_not(stays))
        def _():
            for i in range(PIECES + 1):
                set_remote(i).start()

    def receive_table():
        set_local(0).wait()
        to_table = pltpu.make_async_copy(s.numbers_in, s.table, s.local_sems.at[2])
        to_table.start()
        to_table.wait()

    def receive_piece(i):
        set_local(i + 1).wait()

    def multiply(q, first):
        def four(i, carry):
            base = first + 4 * i
            total = of("products", q)[base]
            for j in range(4):
                block = of("blocks", q)[entry(s.table, 1, base + j, 63)]
                product = jnp.dot(s.tile_set[base + j], block, preferred_element_type=F32)
                total = product + s.table[2, base + j].astype(F32) * total
                of("products", q)[base + j + 1] = total
            return carry

        lax.fori_loop(0, SLOT_STEP // 4, four, 0)

    def multiply_pieces(q, piece):
        for first in range(piece * per_piece, (piece + 1) * per_piece, SLOT_STEP):
            multiply(q, first)

    set_x, set_y = set_of(x, y, zh, core)
    here = (set_x + 4 - x) % 4 == 0

    def to_owner(part, distance):
        there = (y + distance) % 4
        return remote(
            of("partial", part).at[:, there], of("plane_in", part).at[set_y], s.plane_send.at[part, distance],
            s.plane_recv.at[part, set_y], at(set_x, there, zl, zh, core),
        )

    def send_partial(part):
        q, first = SUMS[part]
        for t in range(8):
            sums = of("products", q)[entry(s.table, 3, t, SLOTS), :, first : first + 128]
            of("partial", part)[t // 4, t % 4] = sums.astype(BF16)
        for distance in (2, 1, 3):
            to_owner(part, distance).start()

        @pl.when(here)
        def _():
            pltpu.make_async_copy(
                of("partial", part).at[:, y], of("plane_in", part).at[set_y], s.plane_recv.at[part, set_y]
            ).start()

        when_not(here, lambda: to_owner(part, 0).start())

    def across(part):
        return remote(
            of("z_out", part), of("z_in", part), s.z_send.at[part], s.z_recv.at[part], z_neighbour(x, y, zl, zh, core, 8)
        )

    def sum_plane(part):
        for member in range(4):
            ref = of("plane_in", part).at[member]
            remote(ref, ref, s.plane_send.at[part, 0], s.plane_recv.at[part, member], sibling).wait_recv()

        def summed(half):
            result = of("plane_in", part)[0, half].astype(F32)
            for member in range(1, 4):
                result += of("plane_in", part)[member, half].astype(F32)
            return result

        of("z_out", part)[...] = summed(1 - zh).astype(BF16)
        across(part).start()
        of("own", part)[...] = summed(zh)

    def agg_copy(part, of_core):
        ref = s.agg.at[of_core, :, pl.ds(128 * part, 128)]
        return remote(ref, ref, s.agg_send.at[part], s.agg_recv.at[part], sibling)

    def aggregate(part):
        across(part).wait_recv()
        mine = (of("own", part)[...] + of("z_in", part)[...].astype(F32)).astype(BF16)
        s.agg[core, :, 128 * part : 128 * part + 128] = mine
        agg_copy(part, core).start()
        return jnp.dot(mine, weight[128 * part : 128 * part + 128, :], preferred_element_type=F32)

    def send_sums(q):
        for part, (of_columns, _) in enumerate(SUMS):
            if of_columns == q:
                send_partial(part)

    def drain_features(q):
        @pl.when(is_source)
        def _():
            own_remote(q, 0).wait_send()
            own_remote(q, 1).wait_send()

        for unit in (ALONE, BOTH):
            for upward in (True, False):
                for step in range(hops(q, unit, upward)):
                    hop(q, step, unit, upward).wait_send()
        for distance in (-4, -3, -2, -1, 1, 2, 3):
            y_copy(q, distance, ALONE).wait_send()
            for unit in (ALONE, BOTH, FROM_Y):
                if unit != FROM_Y or distance != -4:
                    pair_copy(q, distance, unit, core).wait_send()
        y_other_copy(q).wait_send()

    def drain_set():
        @pl.when(jnp.logical_not(stays))
        def _():
            for i in range(PIECES + 1):
                set_remote(i).wait_send()

    def drain_sums(part):
        for distance in (1, 2, 3):
            to_owner(part, distance).wait_send()
        when_not(here, lambda: to_owner(part, 0).wait_send())
        across(part).wait_send()
        agg_copy(part, core).wait_send()

    slots = [[] for _ in range(2 * chunks + 4)]
    for q in range(chunks):
        slots[2 * q].append(lambda q=q: own_event(q))
        for step in range(4):
            slots[2 * q + 1 + step] += ring_events(q, step)
            slots[2 * q + 2 + step] += y_events(q, step)

    send_own(0)
    send_set()
    for event in slots.pop(0):
        event()
    for q in range(1, chunks):
        send_own(q)
    for load in loads:
        load.start()
    for q in range(chunks):
        of("products", q)[0] = jnp.zeros((128, WIDTHS[q]), F32)
    for slot, events in enumerate(slots, 1):
        if slot in (2, 4, 6):
            greeted(slot // 2 - 1)
            if slot < 6:
                greet(slot // 2)
        if slot == 6:
            pair_arrivals(0)
            receive_table()
            for piece in (0, 1):
                receive_piece(piece)
                multiply_pieces(0, piece)
        if slot == 7:
            receive_piece(2)
            multiply_pieces(0, 2)
            send_sums(0)
        for event in events:
            event()
    for q in range(1, chunks):
        pair_arrivals(q)
        for piece in range(PIECES):
            multiply_pieces(q, piece)
        if q < chunks - 1:
            send_sums(q)
    send_sums(chunks - 1)
    for q in range(chunks):
        drain_features(q)
    drain_set()
    for load in loads:
        load.wait()
    for part in range(len(SUMS)):
        sum_plane(part)
    pre = aggregate(0)
    for part in range(1, len(SUMS)):
        pre += aggregate(part)

    sigma = jax.nn.sigmoid(pre)
    s.slope[core] = (cotangent[...].astype(F32) * sigma * (1.0 + pre * (1.0 - sigma))).astype(BF16)
    slope_copy = remote(s.slope.at[core], s.slope.at[core], s.slope_sems.at[0], s.slope_sems.at[1], sibling)
    slope_copy.start()
    node_out[...] = (pre * sigma).astype(node_out.dtype)
    for part in range(len(SUMS)):
        agg_copy(part, 1 - core).wait_recv()
    slope_copy.wait_recv()

    columns = pl.ds(pl.multiple_of(core * 256, 256), 256)
    local = lax.dot_general(
        s.agg[:, :, columns].reshape(256, 256), s.slope[...].reshape(256, 512),
        (((0,), (0,)), ((), ())), preferred_element_type=F32,
    )
    s.grad[...] = local.reshape(16, 16, 512).astype(BF16)

    def grad_copy(step):
        there = spot_at(step)
        return remote(
            s.grad.at[there], s.grad_in.at[spot], s.grad_send.at[4 * step[0] + step[1]], s.grad_recv.at[spot],
            in_plane(step),
        )

    for step in FAR_FIRST:
        grad_copy(step).start()
    slope_copy.wait_send()
    for part in range(len(SUMS)):
        drain_sums(part)
    rows_sum = s.grad[spot].astype(F32)
    for step in reversed(FAR_FIRST):
        there = spot_at(step)
        ref = s.grad_in.at[there]
        remote(ref, ref, s.grad_send.at[0], s.grad_recv.at[there], sibling).wait_recv()
        rows_sum += s.grad_in[there].astype(F32)
    for j in range(8):
        s.piece[j] = rows_sum[8 * (j // 4) : 8 * (j // 4) + 8, 128 * (j % 4) : 128 * (j % 4) + 128]

    def piece_copy(distance):
        there = (z + distance) % 16
        return remote(
            s.piece.at[there % 8], s.piece_in.at[z], s.piece_send.at[distance], s.piece_recv.at[z],
            z_neighbour(x, y, zl, zh, core, distance),
        )

    for distance in (8, 7, 9, 6, 10, 5, 11, 4, 12, 3, 13, 2, 14, 1, 15):
        piece_copy(distance).start()
    s.piece_in[z] = s.piece[zl]
    for step in FAR_FIRST:
        grad_copy(step).wait_send()
    for distance in range(1, 16):
        there = (z + distance) % 16
        ref = s.piece_in.at[there]
        remote(ref, ref, s.piece_send.at[0], s.piece_recv.at[there], sibling).wait_recv()
    result = s.piece_in[0]
    for j in range(1, 16):
        result += s.piece_in[j]
    s.total[...] = result
    s.total_in[zl] = result

    def total_copy(distance):
        return remote(
            s.total, s.total_in.at[zl], s.total_send.at[distance + 3], s.total_recv.at[zl],
            z_neighbour(x, y, zl, zh, core, distance),
        )

    near = (4, -3, 3, -2, 2, -1, 1)
    for distance in near:
        total_copy(distance).start()
    for distance in range(1, 16):
        piece_copy(distance).wait_send()
    for distance in range(1, 8):
        there = (zl + distance) % 8
        remote(s.total, s.total_in.at[there], s.total_send.at[0], s.total_recv.at[there], sibling).wait_recv()
    upper = jnp.concatenate([s.total_in[j] for j in range(4)], axis=1)
    lower = jnp.concatenate([s.total_in[j] for j in range(4, 8)], axis=1)
    s.whole[core, spot] = jnp.concatenate([upper, lower], axis=0).astype(BF16)

    def whole_copy(step):
        ref = s.whole.at[core, spot]
        return remote(ref, ref, s.whole_send.at[4 * step[0] + step[1]], s.whole_recv.at[spot], in_plane(step))

    def last_copy(n, of_core):
        ref = s.whole.at[of_core, n]
        return remote(ref, ref, s.last_send.at[n], s.last_recv.at[n], sibling)

    for step in FAR_FIRST:
        whole_copy(step).start()
    last_copy(spot, core).start()
    for distance in near:
        total_copy(distance).wait_send()
    for step in reversed(FAR_FIRST):
        there = spot_at(step)
        ref = s.whole.at[core, there]
        remote(ref, ref, s.whole_send.at[0], s.whole_recv.at[there], sibling).wait_recv()
        last_copy(there, core).start()
    for n in range(16):
        last_copy(n, 1 - core).wait_recv()
    weight_grad[...] = s.whole[...].reshape(512, 512)

    for step in FAR_FIRST:
        whole_copy(step).wait_send()
    for n in range(16):
        last_copy(n, core).wait_send()


def shards(features, tiles, tile_rows, tile_cols, tile_count, weight, cotangent):
    vmem = pl.BlockSpec(memory_space=pltpu.VMEM)
    anywhere = pl.BlockSpec(memory_space=pl.ANY)
    node_out, weight_grad = pl.pallas_call(
        layer_kernel,
        out_shape=(
            jax.ShapeDtypeStruct(cotangent.shape, BF16),
            jax.ShapeDtypeStruct(weight.shape, BF16),
        ),
        in_specs=[anywhere, anywhere, vmem, vmem, vmem, anywhere, anywhere],
        out_specs=(vmem, vmem),
        scratch_shapes=list(scratch().values()),
        compiler_params=pltpu.CompilerParams(
            collective_id=0, has_side_effects=True, vmem_limit_bytes=60 * 2**20
        ),
        name="layer",
    )(
        features.reshape(8, 128, 512), tiles, tile_rows, tile_cols, tile_count, weight, cotangent,
    )
    return node_out, weight_grad.astype(F32)


def solution(mesh):
    in_specs = (
        P("dom", None),
        P(("dom", "rep"), None, None),
        P(("dom", "rep")),
        P(("dom", "rep")),
        P(("dom", "rep")),
        P(),
        P(("dom", "rep"), None),
    )
    out_specs = (P(("dom", "rep"), None), P())
    return jax.shard_map(shards, mesh=mesh, in_specs=in_specs, out_specs=out_specs, check_vma=False)
```

```python
import types

import jax
import jax.numpy as jnp
from jax import lax
from jax.experimental import pallas as pl
from jax.experimental.pallas import tpu as pltpu
from jax.sharding import PartitionSpec as P

MESH = pl.DeviceIdType.MESH
BF16 = jnp.bfloat16
F32 = jnp.float32
I32 = jnp.int32

WIDTHS = (256, 256)
ALONE, BOTH, FROM_Y = range(3)
SUMS = [(q, first) for q, width in enumerate(WIDTHS) for first in range(0, width, 128)]
SLOTS = 48
PIECES = 3
SLOT_STEP = 8
FAR_FIRST = sorted(
    [(dx, dy) for dx in range(4) for dy in range(4) if dx or dy],
    key=lambda d: -min(d[0], 4 - d[0]) - min(d[1], 4 - d[1]),
)


def at(x, y, zl, zh, core):
    return zl * 8 + x * 2 + core, zh * 4 + y


def hosted(x, y, zh, core):
    c = (2 * x + core + 16 - 4 * zh - y) % 8
    member = ((y + 1) // 2) % 2
    return c // 2, (1 - c % 2) * member + (c % 2) * (3 - member)


def set_of(host_x, host_y, zh, core):
    natural_core = host_y // 2
    member = (1 - natural_core) * host_y + natural_core * (3 - host_y)
    other = (core + natural_core) % 2
    y = (1 - other) * 2 * member + other * (3 - 2 * member)
    return ((2 * host_x + natural_core + 4 * zh + y - core) // 2) % 4, y


def place():
    dom, rep = lax.axis_index("dom"), lax.axis_index("rep")
    return (dom // 2) % 4, rep % 4, dom // 8, rep // 4, dom % 2


def z_neighbour(x, y, zl, zh, core, distance):
    z = (zh * 8 + zl + distance + 16) % 16
    return at(x, y, z % 8, z // 8, core)


def signal(device):
    pl.semaphore_signal(pltpu.get_barrier_semaphore(), inc=1, device_id=device, device_id_type=MESH)


def remote(src, dst, send, recv, device):
    return pltpu.make_async_remote_copy(
        src_ref=src, dst_ref=dst, send_sem=send, recv_sem=recv, device_id=device, device_id_type=MESH
    )


def when_not(condition, action):
    pl.when(jnp.logical_not(condition))(action)


def sort_slots(rows, cols, count, numbers):
    shape = (SLOTS, SLOTS)
    sub = lax.broadcasted_iota(I32, shape, 0).astype(F32)
    lane = lax.broadcasted_iota(I32, shape, 1).astype(F32)
    eye = (sub == lane).astype(F32)

    def column(row):
        return jnp.sum(eye * row, axis=1, keepdims=True)

    live = lane[:1] < count[...].reshape(1, 1).astype(F32)
    key = jnp.where(live, rows[...].reshape(1, SLOTS).astype(F32), 8.0)
    col = cols[...].reshape(1, SLOTS)
    block = ((col >> 6) * 8 + (col & 7)).astype(F32)
    unique = key * 64.0 + lane[:1]
    key_column = column(key)
    rank = jnp.sum((unique < column(unique)).astype(F32), axis=1, keepdims=True)
    chosen = (rank == lane).astype(F32)
    after = (rank + 1.0 == lane).astype(F32)
    sorted_key = jnp.sum(chosen * key_column, axis=0, keepdims=True)
    key_before = jnp.sum(after * key_column, axis=0, keepdims=True)
    numbers[0:1, 0:SLOTS] = jnp.sum(chosen * sub, axis=0, keepdims=True).astype(I32)
    numbers[1:2, 0:SLOTS] = jnp.sum(chosen * column(block), axis=0, keepdims=True).astype(I32)
    numbers[2:3, 0:SLOTS] = (sorted_key == key_before).astype(I32)
    ends = jnp.where(key_column == lane, rank + 1.0, 0.0)
    numbers[3:4, 0:SLOTS] = jnp.max(ends, axis=0, keepdims=True).astype(I32)


def scratch():
    vmem, sems = pltpu.VMEM, pltpu.SemaphoreType.DMA
    chunks = len(WIDTHS)
    names = {
        "numbers": vmem((8, 128), I32),
        "numbers_in": vmem((8, 128), I32),
        "own_table": pltpu.SMEM((8, 128), I32),
        "table": pltpu.SMEM((8, 128), I32),
        "tiles": vmem((SLOTS, 128, 128), BF16),
        "sorted_tiles": vmem((SLOTS, 128, 128), BF16),
        "tile_set": vmem((SLOTS, 128, 128), BF16),
        "weight": vmem((512, 512), BF16),
        "cotangent": vmem((128, 512), BF16),
        "load_sems": sems((2,)),
        "line_sems": pltpu.SemaphoreType.REGULAR((3,)),
        "agg": vmem((2, 128, 512), BF16),
        "slope": vmem((2, 128, 512), BF16),
        "grad": vmem((16, 16, 512), BF16),
        "grad_in": vmem((16, 16, 512), BF16),
        "piece": vmem((8, 8, 128), F32),
        "piece_in": vmem((16, 8, 128), F32),
        "total": vmem((8, 128), F32),
        "total_in": vmem((8, 8, 128), F32),
        "whole": vmem((2, 16, 16, 512), BF16),
        "set_send": sems((PIECES + 1,)),
        "set_recv": sems((PIECES + 1,)),
        "local_sems": sems((3,)),
        "own_send": sems((chunks, 2)),
        "own_recv": sems((chunks, 2)),
        "ring_send": sems((chunks, 2, 4, 2)),
        "ring_recv": sems((chunks, 2, 4, 2)),
        "y_send": sems((chunks, 8)),
        "y_recv": sems((chunks, 8)),
        "y_other_send": sems((chunks,)),
        "pair_send": sems((chunks, 8, 3)),
        "pair_recv": sems((chunks, 8, 3)),
        "plane_send": sems((len(SUMS), 4)),
        "plane_recv": sems((len(SUMS), 4)),
        "z_send": sems((len(SUMS),)),
        "z_recv": sems((len(SUMS),)),
        "agg_send": sems((len(SUMS),)),
        "agg_recv": sems((len(SUMS),)),
        "slope_sems": sems((2,)),
        "grad_send": sems((16,)),
        "grad_recv": sems((16,)),
        "piece_send": sems((16,)),
        "piece_recv": sems((16,)),
        "total_send": sems((8,)),
        "total_recv": sems((8,)),
        "whole_send": sems((16,)),
        "whole_recv": sems((16,)),
        "last_send": sems((16,)),
        "last_recv": sems((16,)),
    }
    for q, width in enumerate(WIDTHS):
        names["blocks%d" % q] = vmem((64, 128, width), BF16)
        names["products%d" % q] = vmem((SLOTS + 1, 128, width), F32)
    for part in range(len(SUMS)):
        names["partial%d" % part] = vmem((2, 4, 128, 128), BF16)
        names["plane_in%d" % part] = vmem((4, 2, 128, 128), BF16)
        names["z_out%d" % part] = vmem((128, 128), BF16)
        names["z_in%d" % part] = vmem((128, 128), BF16)
        names["own%d" % part] = vmem((128, 128), F32)
    return names


def layer_kernel(features, tiles_in, rows, cols, count, weight_in, cotangent_in, node_out, weight_grad, *refs):
    s = types.SimpleNamespace(**dict(zip(scratch(), refs)))
    chunks = len(WIDTHS)
    starts = [sum(WIDTHS[:q]) for q in range(chunks)]

    def of(name, q):
        return getattr(s, name + str(q))

    x, y, zl, zh, core = place()
    z = zh * 8 + zl
    spot = x * 4 + y
    sibling = at(x, y, zl, zh, 1 - core)
    up = z_neighbour(x, y, zl, zh, core, 1)
    down = z_neighbour(x, y, zl, zh, core, -1)
    natural_core = y // 2
    is_source = core == natural_core
    member = y % 2
    y_pair = at(x, y + 1 - 2 * member, zl, zh, core)
    y_pair_other = at(x, y + 1 - 2 * member, zl, zh, 1 - core)

    def in_plane(step):
        return at((x + step[0]) % 4, (y + step[1]) % 4, zl, zh, core)

    def spot_at(step):
        return (x + step[0]) % 4 * 4 + (y + step[1]) % 4

    weight, cotangent = s.weight, s.cotangent
    loads = [
        pltpu.make_async_copy(weight_in, weight, s.load_sems.at[0]),
        pltpu.make_async_copy(cotangent_in, cotangent, s.load_sems.at[1]),
    ]
    load_tiles = pltpu.make_async_copy(tiles_in, s.tiles, s.local_sems.at[0])
    load_tiles.start()

    for step in FAR_FIRST:
        signal(in_plane(step))
    signal(up)
    signal(down)
    signal(y_pair_other)
    signal(sibling)
    def entry(table, row, place, top):
        return jnp.minimum(jnp.maximum(table[row, place], 0), top)

    def place_tile(j, carry):
        s.sorted_tiles[j] = s.tiles[entry(s.own_table, 0, j, SLOTS - 1)]
        return carry

    sort_slots(rows, cols, count, s.numbers)
    to_own_table = pltpu.make_async_copy(s.numbers, s.own_table, s.local_sems.at[1])
    to_own_table.start()
    load_tiles.wait()
    to_own_table.wait()
    lax.fori_loop(0, SLOTS, place_tile, 0, unroll=2)

    pl.semaphore_wait(pltpu.get_barrier_semaphore(), 19)

    def greet(i):
        for distance in (2**i, -(2**i)):
            pl.semaphore_signal(
                s.line_sems.at[i], inc=1, device_id=z_neighbour(x, y, zl, zh, core, distance), device_id_type=MESH
            )

    def greeted(i):
        pl.semaphore_wait(s.line_sems.at[i], 2)

    greet(0)

    def block_rows(distance, of_core):
        return (zl + distance + 8) % 8 * 8 + of_core * 4

    def block_part(q, distance, unit, of_core):
        row = block_rows(distance, of_core)
        row = row + (member if unit == ALONE else 2 if unit == BOTH else 1 - member)
        return of("blocks", q).at[pl.ds(row, 2 if unit == BOTH else 1)]

    def own_part(q, of_core):
        columns = pl.ds(starts[q], WIDTHS[q])
        return features.at[pl.ds(of_core * 4, 4), :, columns], of("blocks", q).at[pl.ds(block_rows(0, of_core), 4)]

    def own_local(q, of_core):
        return pltpu.make_async_copy(*own_part(q, of_core), s.own_recv.at[q, of_core])

    def own_remote(q, of_core):
        return remote(*own_part(q, of_core), s.own_send.at[q, of_core], s.own_recv.at[q, of_core], sibling)

    def send_own(q):
        @pl.when(is_source)
        def _():
            own_remote(q, 1 - core).start()
            own_local(q, core).start()
            own_remote(q, core).start()
            own_local(q, 1 - core).start()

    def hop(q, step, unit, upward):
        ref = block_part(q, -step if upward else step, unit, core)
        way = 0 if upward else 1
        return remote(
            ref, ref, s.ring_send.at[q, way, step, unit], s.ring_recv.at[q, way, step, unit], up if upward else down
        )

    def arrival(q, step, unit, upward):
        ref = block_part(q, -step - 1 if upward else step + 1, unit, core)
        way = 0 if upward else 1
        return remote(ref, ref, s.ring_send.at[q, way, step, unit], s.ring_recv.at[q, way, step, unit], sibling)

    def y_copy(q, distance, unit):
        ref = block_part(q, distance, unit, core)
        return remote(ref, ref, s.y_send.at[q, distance + 4], s.y_recv.at[q, distance + 4], y_pair)

    def y_other_copy(q):
        ref = block_part(q, -4, ALONE, core)
        return remote(ref, ref, s.y_other_send.at[q], s.pair_recv.at[q, 0, FROM_Y], y_pair_other)

    def pair_copy(q, distance, unit, of_core):
        ref = block_part(q, distance, unit, of_core)
        return remote(ref, ref, s.pair_send.at[q, distance + 4, unit], s.pair_recv.at[q, distance + 4, unit], sibling)

    def hops(q, unit, upward):
        return 4 if (unit == (ALONE if q % 2 == 0 else BOTH)) == upward else 3

    def own_event(q):
        own_local(q, core).wait()
        for unit in (ALONE, BOTH):
            hop(q, 0, unit, True).start()
            hop(q, 0, unit, False).start()

    def ring_event(q, step, unit, upward):
        arrival(q, step, unit, upward).wait_recv()
        if step + 1 < hops(q, unit, upward):
            hop(q, step + 1, unit, upward).start()
        distance = -step - 1 if upward or step == 3 else step + 1
        if unit == ALONE:
            y_copy(q, distance, ALONE).start()
            if distance == -4:
                y_other_copy(q).start()
        pair_copy(q, distance, unit, core).start()

    def y_event(q, distance):
        y_copy(q, distance, FROM_Y).wait_recv()
        if distance != -4:
            pair_copy(q, distance, FROM_Y, core).start()

    def ring_events(q, step):
        return [
            lambda unit=unit, upward=upward: ring_event(q, step, unit, upward)
            for unit in (ALONE, BOTH)
            for upward in (True, False)
            if step < hops(q, unit, upward)
        ]

    def y_events(q, step):
        distances = (-4,) if step == 3 else (-step - 1, step + 1)
        return [lambda distance=distance: y_event(q, distance) for distance in distances]

    def pair_arrivals(q):
        own_local(q, 1 - core).wait()
        for distance in (-1, 1, -2, 2, -3, 3, -4):
            for unit in (ALONE, BOTH, FROM_Y):
                pair_copy(q, distance, unit, 1 - core).wait_recv()

    host_x, host_y = hosted(x, y, zh, core)
    stays = (host_x + 4 - x) % 4 + (host_y + 4 - y) % 4 == 0
    host = at(host_x, host_y, zl, zh, core)
    per_piece = SLOTS // PIECES
    set_parts = [(s.numbers, s.numbers_in)] + [
        (s.sorted_tiles.at[pl.ds(i * per_piece, per_piece)], s.tile_set.at[pl.ds(i * per_piece, per_piece)])
        for i in range(PIECES)
    ]

    def set_remote(i):
        return remote(*set_parts[i], s.set_send.at[i], s.set_recv.at[i], host)

    def set_local(i):
        return pltpu.make_async_copy(*set_parts[i], s.set_recv.at[i])

    def send_set():
        @pl.when(stays)
        def _():
            for i in range(PIECES + 1):
                set_local(i).start()

        @pl.when(jnp.logical_not(stays))
        def _():
            for i in range(PIECES + 1):
                set_remote(i).start()

    def receive_table():
        set_local(0).wait()
        to_table = pltpu.make_async_copy(s.numbers_in, s.table, s.local_sems.at[2])
        to_table.start()
        to_table.wait()

    def receive_piece(i):
        set_local(i + 1).wait()

    def multiply(q, first):
        def four(i, carry):
            base = first + 4 * i
            total = of("products", q)[base]
            for j in range(4):
                block = of("blocks", q)[entry(s.table, 1, base + j, 63)]
                product = jnp.dot(s.tile_set[base + j], block, preferred_element_type=F32)
                total = product + s.table[2, base + j].astype(F32) * total
                of("products", q)[base + j + 1] = total
            return carry

        lax.fori_loop(0, SLOT_STEP // 4, four, 0)

    def multiply_pieces(q, piece):
        for first in range(piece * per_piece, (piece + 1) * per_piece, SLOT_STEP):
            multiply(q, first)

    set_x, set_y = set_of(x, y, zh, core)
    here = (set_x + 4 - x) % 4 == 0

    def to_owner(part, distance):
        there = (y + distance) % 4
        return remote(
            of("partial", part).at[:, there], of("plane_in", part).at[set_y], s.plane_send.at[part, distance],
            s.plane_recv.at[part, set_y], at(set_x, there, zl, zh, core),
        )

    def send_partial(part):
        q, first = SUMS[part]
        for t in range(8):
            sums = of("products", q)[entry(s.table, 3, t, SLOTS), :, first : first + 128]
            of("partial", part)[t // 4, t % 4] = sums.astype(BF16)
        for distance in (2, 1, 3):
            to_owner(part, distance).start()

        @pl.when(here)
        def _():
            pltpu.make_async_copy(
                of("partial", part).at[:, y], of("plane_in", part).at[set_y], s.plane_recv.at[part, set_y]
            ).start()

        when_not(here, lambda: to_owner(part, 0).start())

    def across(part):
        return remote(
            of("z_out", part), of("z_in", part), s.z_send.at[part], s.z_recv.at[part], z_neighbour(x, y, zl, zh, core, 8)
        )

    def sum_plane(part):
        for member in range(4):
            ref = of("plane_in", part).at[member]
            remote(ref, ref, s.plane_send.at[part, 0], s.plane_recv.at[part, member], sibling).wait_recv()

        def summed(half):
            result = of("plane_in", part)[0, half].astype(F32)
            for member in range(1, 4):
                result += of("plane_in", part)[member, half].astype(F32)
            return result

        of("z_out", part)[...] = summed(1 - zh).astype(BF16)
        across(part).start()
        of("own", part)[...] = summed(zh)

    def agg_copy(part, of_core):
        ref = s.agg.at[of_core, :, pl.ds(128 * part, 128)]
        return remote(ref, ref, s.agg_send.at[part], s.agg_recv.at[part], sibling)

    def aggregate(part):
        across(part).wait_recv()
        mine = (of("own", part)[...] + of("z_in", part)[...].astype(F32)).astype(BF16)
        s.agg[core, :, 128 * part : 128 * part + 128] = mine
        agg_copy(part, core).start()
        return jnp.dot(mine, weight[128 * part : 128 * part + 128, :], preferred_element_type=F32)

    def send_sums(q):
        for part, (of_columns, _) in enumerate(SUMS):
            if of_columns == q:
                send_partial(part)

    def drain_features(q):
        @pl.when(is_source)
        def _():
            own_remote(q, 0).wait_send()
            own_remote(q, 1).wait_send()

        for unit in (ALONE, BOTH):
            for upward in (True, False):
                for step in range(hops(q, unit, upward)):
                    hop(q, step, unit, upward).wait_send()
        for distance in (-4, -3, -2, -1, 1, 2, 3):
            y_copy(q, distance, ALONE).wait_send()
            for unit in (ALONE, BOTH, FROM_Y):
                if unit != FROM_Y or distance != -4:
                    pair_copy(q, distance, unit, core).wait_send()
        y_other_copy(q).wait_send()

    def drain_set():
        @pl.when(jnp.logical_not(stays))
        def _():
            for i in range(PIECES + 1):
                set_remote(i).wait_send()

    def drain_sums(part):
        for distance in (1, 2, 3):
            to_owner(part, distance).wait_send()
        when_not(here, lambda: to_owner(part, 0).wait_send())
        across(part).wait_send()
        agg_copy(part, core).wait_send()

    slots = [[] for _ in range(2 * chunks + 4)]
    for q in range(chunks):
        slots[2 * q].append(lambda q=q: own_event(q))
        for step in range(4):
            slots[2 * q + 1 + step] += ring_events(q, step)
            slots[2 * q + 2 + step] += y_events(q, step)

    send_own(0)
    send_set()
    for event in slots.pop(0):
        event()
    for q in range(1, chunks):
        send_own(q)
    for load in loads:
        load.start()
    for q in range(chunks):
        of("products", q)[0] = jnp.zeros((128, WIDTHS[q]), F32)
    for slot, events in enumerate(slots, 1):
        if slot in (2, 4, 6):
            greeted(slot // 2 - 1)
            if slot < 6:
                greet(slot // 2)
        if slot == 6:
            pair_arrivals(0)
            receive_table()
            for piece in (0, 1):
                receive_piece(piece)
                multiply_pieces(0, piece)
        if slot == 7:
            receive_piece(2)
            multiply_pieces(0, 2)
            send_sums(0)
        for event in events:
            event()
    for q in range(1, chunks):
        pair_arrivals(q)
        for piece in range(PIECES):
            multiply_pieces(q, piece)
        if q < chunks - 1:
            send_sums(q)
    send_sums(chunks - 1)
    for q in range(chunks):
        drain_features(q)
    drain_set()
    for load in loads:
        load.wait()
    for part in range(len(SUMS)):
        sum_plane(part)
    pre = aggregate(0)
    for part in range(1, len(SUMS)):
        pre += aggregate(part)

    sigma = jax.nn.sigmoid(pre)
    s.slope[core] = (cotangent[...].astype(F32) * sigma * (1.0 + pre * (1.0 - sigma))).astype(BF16)
    slope_copy = remote(s.slope.at[core], s.slope.at[core], s.slope_sems.at[0], s.slope_sems.at[1], sibling)
    slope_copy.start()
    node_out[...] = (pre * sigma).astype(node_out.dtype)
    for part in range(len(SUMS)):
        agg_copy(part, 1 - core).wait_recv()
    slope_copy.wait_recv()

    columns = pl.ds(pl.multiple_of(core * 256, 256), 256)
    local = lax.dot_general(
        s.agg[:, :, columns].reshape(256, 256), s.slope[...].reshape(256, 512),
        (((0,), (0,)), ((), ())), preferred_element_type=F32,
    )
    s.grad[...] = local.reshape(16, 16, 512).astype(BF16)

    def grad_copy(step):
        there = spot_at(step)
        return remote(
            s.grad.at[there], s.grad_in.at[spot], s.grad_send.at[4 * step[0] + step[1]], s.grad_recv.at[spot],
            in_plane(step),
        )

    for step in FAR_FIRST:
        grad_copy(step).start()
    slope_copy.wait_send()
    for part in range(len(SUMS)):
        drain_sums(part)
    rows_sum = s.grad[spot].astype(F32)
    for step in reversed(FAR_FIRST):
        there = spot_at(step)
        ref = s.grad_in.at[there]
        remote(ref, ref, s.grad_send.at[0], s.grad_recv.at[there], sibling).wait_recv()
        rows_sum += s.grad_in[there].astype(F32)
    for j in range(8):
        s.piece[j] = rows_sum[8 * (j // 4) : 8 * (j // 4) + 8, 128 * (j % 4) : 128 * (j % 4) + 128]

    def piece_copy(distance):
        there = (z + distance) % 16
        return remote(
            s.piece.at[there % 8], s.piece_in.at[z], s.piece_send.at[distance], s.piece_recv.at[z],
            z_neighbour(x, y, zl, zh, core, distance),
        )

    for distance in (8, 7, 9, 6, 10, 5, 11, 4, 12, 3, 13, 2, 14, 1, 15):
        piece_copy(distance).start()
    s.piece_in[z] = s.piece[zl]
    for step in FAR_FIRST:
        grad_copy(step).wait_send()
    for distance in range(1, 16):
        there = (z + distance) % 16
        ref = s.piece_in.at[there]
        remote(ref, ref, s.piece_send.at[0], s.piece_recv.at[there], sibling).wait_recv()
    result = s.piece_in[0]
    for j in range(1, 16):
        result += s.piece_in[j]
    s.total[...] = result
    s.total_in[zl] = result

    def total_copy(distance):
        return remote(
            s.total, s.total_in.at[zl], s.total_send.at[distance + 3], s.total_recv.at[zl],
            z_neighbour(x, y, zl, zh, core, distance),
        )

    near = (4, -3, 3, -2, 2, -1, 1)
    for distance in near:
        total_copy(distance).start()
    for distance in range(1, 16):
        piece_copy(distance).wait_send()
    for distance in range(1, 8):
        there = (zl + distance) % 8
        remote(s.total, s.total_in.at[there], s.total_send.at[0], s.total_recv.at[there], sibling).wait_recv()
    upper = jnp.concatenate([s.total_in[j] for j in range(4)], axis=1)
    lower = jnp.concatenate([s.total_in[j] for j in range(4, 8)], axis=1)
    s.whole[core, spot] = jnp.concatenate([upper, lower], axis=0).astype(BF16)

    def whole_copy(step):
        ref = s.whole.at[core, spot]
        return remote(ref, ref, s.whole_send.at[4 * step[0] + step[1]], s.whole_recv.at[spot], in_plane(step))

    def last_copy(n, of_core):
        ref = s.whole.at[of_core, n]
        return remote(ref, ref, s.last_send.at[n], s.last_recv.at[n], sibling)

    for step in FAR_FIRST:
        whole_copy(step).start()
    last_copy(spot, core).start()
    for distance in near:
        total_copy(distance).wait_send()
    for step in reversed(FAR_FIRST):
        there = spot_at(step)
        ref = s.whole.at[core, there]
        remote(ref, ref, s.whole_send.at[0], s.whole_recv.at[there], sibling).wait_recv()
        last_copy(there, core).start()
    for n in range(16):
        last_copy(n, 1 - core).wait_recv()
    weight_grad[...] = s.whole[...].reshape(512, 512)

    for step in FAR_FIRST:
        whole_copy(step).wait_send()
    for n in range(16):
        last_copy(n, core).wait_send()


def shards(features, tiles, tile_rows, tile_cols, tile_count, weight, cotangent):
    vmem = pl.BlockSpec(memory_space=pltpu.VMEM)
    anywhere = pl.BlockSpec(memory_space=pl.ANY)
    node_out, weight_grad = pl.pallas_call(
        layer_kernel,
        out_shape=(
            jax.ShapeDtypeStruct(cotangent.shape, BF16),
            jax.ShapeDtypeStruct(weight.shape, BF16),
        ),
        in_specs=[anywhere, anywhere, vmem, vmem, vmem, anywhere, anywhere],
        out_specs=(vmem, vmem),
        scratch_shapes=list(scratch().values()),
        compiler_params=pltpu.CompilerParams(
            collective_id=0, has_side_effects=True, vmem_limit_bytes=60 * 2**20
        ),
        name="layer",
    )(
        features.reshape(8, 128, 512), tiles, tile_rows, tile_cols, tile_count, weight, cotangent,
    )
    return node_out, weight_grad.astype(F32)


def solution(mesh):
    in_specs = (
        P("dom", None),
        P(("dom", "rep"), None, None),
        P(("dom", "rep")),
        P(("dom", "rep")),
        P(("dom", "rep")),
        P(),
        P(("dom", "rep"), None),
    )
    out_specs = (P(("dom", "rep"), None), P())
    return jax.shard_map(shards, mesh=mesh, in_specs=in_specs, out_specs=out_specs, check_vma=False)
```
